512 devices in a mesh: epoch: 32 (over z, core), row: 4 (over x), col: 4 (over y).
Axes of the slice: x: 4, y: 4, z: 16, core: 2. Of those that a mesh axis runs over, the one named last changes fastest.
Arguments:
- slc_images: bfloat16 [64, 2, 256, 4096], P('epoch', None, 'row', 'col'), may hold values from -3 to 3, as said below
- pair_list: int32 [128, 2], replicated, may hold values from 0 to 63, as said below
- look_sizes: int32 [128, 2], P('epoch'), may hold values from 2 to 8, as said below
Outputs:
- interferogram: float32 [128, 2, 256, 4096], P('epoch', None, 'row', 'col')
- coherence: float32 [128, 256, 4096], P('epoch', 'row', 'col')
The draws below stay inside these ranges and needn't reach their ends.
Inputs may be any that keep to these rules, and one draw needn't show every extreme that they name: `slc_images`: every pixel's magnitude lies between 0.3 and 3. `pair_list`: pair p's reference lies in aligned block b = p // 4 of 2 acquisitions. For p % 4 == 1 the secondary lies in block (b + 32 / 2) modulo 32; for the other pairs it is 1 to 2 acquisitions later, or, where that passes the last acquisition, as many earlier, and for p % 4 == 0 exactly 2 away. `look_sizes`: row half widths run from 2, column half widths from 4; some pair has 8 in both.
All inputs are finite; a program needn't handle non-finite values.
Results may differ from the reference program's by a relative error of at most 0.0003.
Values may be sent and summed in bfloat16 or wider, within the bound.
No kernel may reach another device: no remote copies, remote signals or barrier semaphores. Data moves between devices by JAX's collectives and lax.ppermute only.
A program may use at most 64 MiB of HBM per device.

```python
from functools import partial
import jax
import jax.numpy as jnp
from jax import lax

EP_DEV = 2
PAIR_DEV = 4
HALO = 8
EPOCHS = 64
PAIRS = 128
ROWS = 256
COLS = 4096
N_EPOCH = 32


def draw_slc_images(key, part):
    key = jax.random.fold_in(key, 11)
    keys = jax.random.split(key, 4)
    scene = jax.random.uniform(keys[0], (1, ROWS, COLS), jnp.float32, -3.14159, 3.14159)
    spread = jax.random.uniform(keys[1], (EPOCHS, 1, 1), jnp.float32, 0.2, 1.2)
    magnitude = 0.3 * 10.0 ** jax.random.uniform(keys[3], (EPOCHS, ROWS, COLS), jnp.float32)
    phase = scene + spread * jax.random.normal(keys[2], (EPOCHS, ROWS, COLS), jnp.float32)
    stacked = jnp.stack([magnitude * jnp.cos(phase), magnitude * jnp.sin(phase)], axis=1)
    return jnp.clip(stacked, -3.0, 3.0).astype(jnp.bfloat16)


def block_pairs(key, index):
    keys = jax.random.split(key, 3)
    base = index * EP_DEV
    first = base + jax.random.randint(keys[0], (PAIR_DEV,), 0, EP_DEV)
    delta = jax.random.randint(keys[1], (PAIR_DEV,), 1, EP_DEV + 1).at[0].set(EP_DEV)
    forward = first + delta
    second = jnp.where(forward < EPOCHS, forward, first - delta)
    far_block = (index + N_EPOCH // 2) % N_EPOCH
    far_second = far_block * EP_DEV + jax.random.randint(keys[2], (), 0, EP_DEV)
    second = second.at[1].set(far_second)
    return jnp.stack([first, second], axis=1)


def draw_pair_list(key, part):
    key = jax.random.fold_in(key, 12)
    keys = jax.random.split(key, N_EPOCH)
    indices = jnp.arange(N_EPOCH, dtype=jnp.int32)
    return jax.vmap(block_pairs)(keys, indices).reshape(PAIRS, 2).astype(jnp.int32)


def draw_look_sizes(key, part):
    key = jax.random.fold_in(key, 13)
    keys = jax.random.split(key, 2)
    half_rows = jax.random.randint(keys[0], (PAIRS,), 2, HALO + 1)
    half_cols = jax.random.randint(keys[1], (PAIRS,), 4, HALO + 1)
    looks = jnp.stack([half_rows, half_cols], axis=1)
    return looks.at[0].set(HALO).astype(jnp.int32)


def setup_inputs(seed: int = 0) -> dict:
    key_of = jax.random.split(jax.random.key(seed), 4)
    slc_images = draw_slc_images(jax.random.fold_in(key_of[3], 71), 0)
    pair_list = draw_pair_list(jax.random.fold_in(key_of[3], 71), 0)
    look_sizes = draw_look_sizes(jax.random.fold_in(key_of[3], 71), 0)
    return {"slc_images": slc_images, "pair_list": pair_list, "look_sizes": look_sizes}


def box_filter(field, half_rows, half_cols):
    padded = jnp.pad(field, ((HALO, HALO), (HALO, HALO)))
    by_rows = jnp.zeros((ROWS, COLS + 2 * HALO), jnp.float32)
    for offset in range(-HALO, HALO + 1):
        weight = (jnp.abs(offset) <= half_rows).astype(jnp.float32)
        by_rows = by_rows + weight * padded[HALO + offset:HALO + offset + ROWS, :]
    total = jnp.zeros((ROWS, COLS), jnp.float32)
    for offset in range(-HALO, HALO + 1):
        weight = (jnp.abs(offset) <= half_cols).astype(jnp.float32)
        total = total + weight * by_rows[:, HALO + offset:HALO + offset + COLS]
    return total

def one_pair(slc_images, inputs):
    pair, looks = inputs
    first = lax.dynamic_index_in_dim(slc_images, pair[0], 0, keepdims=False).astype(jnp.float32)
    second = lax.dynamic_index_in_dim(slc_images, pair[1], 0, keepdims=False).astype(jnp.float32)
    ref_re, ref_im = (first[0], first[1])
    sec_re, sec_im = (second[0], second[1])
    fields = [ref_re * sec_re + ref_im * sec_im, ref_im * sec_re - ref_re * sec_im, ref_re * ref_re + ref_im * ref_im, sec_re * sec_re + sec_im * sec_im]
    box_sums = [box_filter(field, looks[0], looks[1]) for field in fields]
    window = ((2 * looks[0] + 1) * (2 * looks[1] + 1)).astype(jnp.float32)
    inter = jnp.stack([box_sums[0] / window, box_sums[1] / window])
    coher = jnp.sqrt(box_sums[0] ** 2 + box_sums[1] ** 2) / jnp.sqrt(box_sums[2] * box_sums[3])
    return (inter, coher)

def reference(slc_images, pair_list, look_sizes):
    return lax.map(partial(one_pair, slc_images), (pair_list, look_sizes))
```

```python
import functools

import jax
import jax.numpy as jnp
from jax import lax
from jax.experimental import pallas as pl
from jax.experimental.pallas import tpu as pltpu
from jax.sharding import PartitionSpec as P

HALO = 8
LANES = 128
ROWS = 64
COLS = 1024
BLOCKS = COLS // LANES
PADDED = ROWS + 2 * HALO
F32 = jnp.float32
BF16 = jnp.bfloat16
VMEM_LIMIT = 48 * 1024 * 1024


def lane_iota(rows):
    return lax.broadcasted_iota(jnp.int32, (rows, LANES), 1)


def move_strip(values, source, target):
    return pltpu.roll(values, (target - source) % LANES, 1)


def put_strip(total, values, source, target):
    lane = lane_iota(values.shape[0])
    inside = (lane >= target) & (lane < target + HALO)
    return jnp.where(inside, move_strip(values, source, target), total)


def block(index):
    return slice(index * LANES, (index + 1) * LANES)


def far_lane(part, field, side):
    return HALO * (part * 4 + field * 2 + side)


def split_far_kernel(which, images, border, inner):
    lead = which[0]
    strips = jnp.zeros((16, LANES), F32)
    for column in range(BLOCKS):
        for field in range(2):
            values = images[lead, field, :, block(column)].astype(F32)
            rows = jnp.concatenate([values[:HALO], values[ROWS - HALO :]], axis=0)
            border[pl.ds(column * 32 + field * 16, 16), :] = rows.astype(BF16)
            inner[field, :, block(column)] = values[HALO : ROWS - HALO].astype(BF16)
            for side, at in ((0, 0), (1, BLOCKS - 1)):
                if column == at:
                    for part in range(3):
                        begin = HALO + 16 * part
                        strips = put_strip(
                            strips,
                            values[begin : begin + 16],
                            side * (LANES - HALO),
                            far_lane(part, field, side),
                        )
    border[pl.ds(BLOCKS * 32, 16), :] = strips.astype(BF16)


def top_and_bottom(images, chip_next, far_next, border, acquisition, field, column):
    if acquisition < 4:
        if acquisition < 2:
            first = images[acquisition, field, :16, block(column)].astype(F32)
            last = images[acquisition, field, ROWS - 16 :, block(column)].astype(F32)
        else:
            k = acquisition - 2
            first = chip_next[k, field, :16, block(column)].astype(F32) + far_next[
                k, field, :16, block(column)
            ].astype(F32)
            last = chip_next[k, field, ROWS - 16 :, block(column)].astype(F32) + far_next[
                k, field, ROWS - 16 :, block(column)
            ].astype(F32)
        return first[:HALO], last[HALO:]
    rows = border[pl.ds(column * 32 + field * 16, 16), :].astype(F32)
    return rows[:HALO], rows[HALO:]


def pack_rows_kernel(images, chip_next, far_next, border, up, down):
    for acquisition in range(5):
        at = pl.ds(acquisition * 16, 16)
        for column in range(BLOCKS):
            tops, bottoms = [], []
            for field in range(2):
                top, bottom = top_and_bottom(
                    images, chip_next, far_next, border, acquisition, field, column
                )
                tops.append(top)
                bottoms.append(bottom)
            up[at, block(column)] = jnp.concatenate(tops, axis=0).astype(BF16)
            down[at, block(column)] = jnp.concatenate(bottoms, axis=0).astype(BF16)


def halo_rows(above, below, acquisition, field, column):
    at = pl.ds(acquisition * 16, 16)
    rows = slice(field * HALO, (field + 1) * HALO)
    return (
        above[at, block(column)].astype(F32)[rows],
        below[at, block(column)].astype(F32)[rows],
    )


def pack_columns_kernel(images, chip_next, far_next, border, above, below, left, right):
    strips = border[pl.ds(BLOCKS * 32, 16), :].astype(F32)
    totals = [jnp.zeros((PADDED, LANES), F32), jnp.zeros((PADDED, LANES), F32)]
    for acquisition in range(5):
        for field in range(2):
            target = HALO * (2 * acquisition + field)
            for side, column in ((0, 0), (1, BLOCKS - 1)):
                source = side * (LANES - HALO)
                before, after = halo_rows(above, below, acquisition, field, column)
                if acquisition < 2:
                    main = images[acquisition, field, :, block(column)].astype(F32)
                elif acquisition < 4:
                    k = acquisition - 2
                    main = chip_next[k, field, :, block(column)].astype(F32) + far_next[
                        k, field, :, block(column)
                    ].astype(F32)
                else:
                    rows = border[pl.ds(column * 32 + field * 16, 16), :].astype(F32)
                    inner = [
                        move_strip(strips, far_lane(part, field, side), source)
                        for part in range(3)
                    ]
                    main = jnp.concatenate([rows[:HALO], *inner, rows[HALO:]], axis=0)
                values = jnp.concatenate([before, main, after], axis=0)
                totals[side] = put_strip(totals[side], values, source, target)
    left[...] = totals[0].astype(BF16)
    right[...] = totals[1].astype(BF16)


def halo_block(from_left, from_right, acquisition, field):
    source = HALO * (2 * acquisition + field)
    blank = jnp.zeros((PADDED, LANES), F32)
    after = put_strip(blank, from_right[...].astype(F32), source, 0)
    return put_strip(after, from_left[...].astype(F32), source, LANES - HALO)


def box_sums(reference, secondary, looks, products, sums, write):
    half_rows, half_cols = looks
    for column in range(BLOCKS + 1):
        at = block(column)
        a, b = reference(0, at), reference(1, at)
        c, d = secondary(0, at), secondary(1, at)
        fields = (a * c + b * d, b * c - a * d, a * a + b * b, c * c + d * d)
        for f, value in enumerate(fields):
            high = value.astype(BF16)
            products[f, :PADDED, at] = high
            products[f, PADDED:, at] = (value - high.astype(F32)).astype(BF16)
    inner = lax.broadcasted_iota(jnp.int32, (ROWS, 2 * PADDED), 0)
    outer = lax.broadcasted_iota(jnp.int32, (ROWS, 2 * PADDED), 1)
    outer = jnp.where(outer >= PADDED, outer - PADDED, outer)
    row_band = (jnp.abs(outer - HALO - inner) <= half_rows).astype(F32).astype(BF16)
    outer = lax.broadcasted_iota(jnp.int32, (4 * LANES, 2 * LANES), 0)
    inner = lax.broadcasted_iota(jnp.int32, (4 * LANES, 2 * LANES), 1)
    col_band = (jnp.abs(outer - LANES - inner) <= half_cols).astype(F32).astype(BF16)
    for f in range(4):
        by_rows = jnp.dot(row_band, products[f], preferred_element_type=F32)
        high = by_rows.astype(BF16)
        low = (by_rows - high.astype(F32)).astype(BF16)
        for part, value in ((0, high), (1, low)):
            at = slice((2 * f + part) * ROWS, (2 * f + part + 1) * ROWS)
            sums[at, LANES : LANES + COLS] = value[:, :COLS]
            sums[at, :LANES] = value[:, COLS:]
            sums[at, LANES + COLS :] = value[:, COLS:]
    window = ((2 * half_rows + 1) * (2 * half_cols + 1)).astype(F32)
    scale = 1.0 / jnp.full((ROWS, 2 * LANES), window, F32)
    for j in range(BLOCKS // 2):
        both = jnp.dot(
            sums[:, j * 256 : j * 256 + 512], col_band, preferred_element_type=F32
        )
        real, imag, power, other = (
            both[2 * f * ROWS : (2 * f + 1) * ROWS] + both[(2 * f + 1) * ROWS : (2 * f + 2) * ROWS]
            for f in range(4)
        )
        coherence = jnp.sqrt(real * real + imag * imag) / jnp.sqrt(power * other)
        write(slice(j * 256, (j + 1) * 256), real * scale, imag * scale, coherence)


def near_kernel(
    table, images, chip_next, far_next, above, below, from_left, from_right,
    interferogram, coherence, staged, products, sums,
):
    step = pl.program_id(0)

    @pl.when(step == 0)
    def _():
        for acquisition in range(4):
            for field in range(2):
                for column in range(BLOCKS):
                    before, after = halo_rows(above, below, acquisition, field, column)
                    if acquisition < 2:
                        main = images[acquisition, field, :, block(column)].astype(F32)
                    else:
                        k = acquisition - 2
                        main = chip_next[k, field, :, block(column)].astype(F32) + far_next[
                            k, field, :, block(column)
                        ].astype(F32)
                    staged[acquisition, field, :, block(column)] = jnp.concatenate(
                        [before, main, after], axis=0
                    )
                staged[acquisition, field, :, block(BLOCKS)] = halo_block(
                    from_left, from_right, acquisition, field
                )

    pair = jnp.where(step == 0, 0, step + 1)
    first, second = table[pair, 0], table[pair, 1]

    def write(at, real, imag, value):
        interferogram[0, 0, :, at] = real
        interferogram[0, 1, :, at] = imag
        coherence[0, :, at] = value

    box_sums(
        lambda field, at: staged[first, field, :, at],
        lambda field, at: staged[second, field, :, at],
        (table[pair, 2], table[pair, 3]),
        products,
        sums,
        write,
    )


def far_kernel(
    table, images, border, inner, above, below, from_left, from_right, _, __,
    interferogram, coherence, staged, products, sums,
):
    first = table[1, 0]
    for acquisition in range(2):

        @pl.when(first == acquisition)
        def _(acquisition=acquisition):
            for field in range(2):
                for column in range(BLOCKS):
                    before, after = halo_rows(above, below, acquisition, field, column)
                    main = images[acquisition, field, :, block(column)].astype(F32)
                    staged[0, field, :, block(column)] = jnp.concatenate(
                        [before, main, after], axis=0
                    )
                staged[0, field, :, block(BLOCKS)] = halo_block(
                    from_left, from_right, acquisition, field
                )

    for field in range(2):
        for column in range(BLOCKS):
            before, after = halo_rows(above, below, 4, field, column)
            rows = border[pl.ds(column * 32 + field * 16, 16), :].astype(F32)
            main = inner[field, :, block(column)].astype(F32)
            staged[1, field, :, block(column)] = jnp.concatenate(
                [before, rows[:HALO], main, rows[HALO:], after], axis=0
            )
        staged[1, field, :, block(BLOCKS)] = halo_block(from_left, from_right, 4, field)

    def write(at, real, imag, value):
        interferogram[0, 0, :, at] = real
        interferogram[0, 1, :, at] = imag
        coherence[0, :, at] = value

    box_sums(
        lambda field, at: staged[0, field, :, at],
        lambda field, at: staged[1, field, :, at],
        (table[1, 2], table[1, 3]),
        products,
        sums,
        write,
    )


VMEM = pl.BlockSpec(memory_space=pltpu.VMEM)
SMEM = pl.BlockSpec(memory_space=pltpu.SMEM)
PARAMS = pltpu.CompilerParams(vmem_limit_bytes=VMEM_LIMIT)


def shape(dims, dtype=BF16):
    return jax.ShapeDtypeStruct(dims, dtype)


def scratch(acquisitions):
    return [
        pltpu.VMEM((acquisitions, 2, PADDED, COLS + LANES), F32),
        pltpu.VMEM((4, 2 * PADDED, COLS + LANES), BF16),
        pltpu.VMEM((8 * ROWS, COLS + 2 * LANES), BF16),
    ]


def exchange(first, last, axis):
    peers = lax.axis_size(axis)
    up = [(i, i + 1) for i in range(peers - 1)]
    down = [(j, i) for i, j in up]
    return lax.ppermute(last, axis, up), lax.ppermute(first, axis, down)


def body(slc_images, pair_list, look_sizes):
    groups = lax.axis_size("epoch")
    half = groups // 2
    myself = lax.axis_index("epoch")

    inside = [(b + 1, b) for b in range(0, groups, 2)] + [(groups - 2, groups - 1)]
    across = [(b + 1, b) for b in range(1, groups - 1, 2)]
    far_next = lax.ppermute(slc_images, "epoch", across)

    asker = (myself + half) % groups
    asked = lax.dynamic_slice(pair_list, (4 * asker + 1, 1), (1, 1))[0] - 2 * myself
    border, inner = pl.pallas_call(
        split_far_kernel,
        in_specs=[SMEM, VMEM],
        out_specs=[VMEM, VMEM],
        out_shape=[
            shape((BLOCKS * 32 + 16, LANES)),
            shape((2, ROWS - 2 * HALO, COLS)),
        ],
        compiler_params=PARAMS,
        name="split_far",
    )(asked, slc_images)
    swap = [(b, (b + half) % groups) for b in range(groups)]
    border = lax.ppermute(border, "epoch", swap)
    inner = lax.ppermute(inner, "epoch", swap)

    chip_next = lax.ppermute(slc_images, "epoch", inside)

    up, down = pl.pallas_call(
        pack_rows_kernel,
        in_specs=[VMEM] * 4,
        out_specs=[VMEM, VMEM],
        out_shape=[shape((80, COLS))] * 2,
        compiler_params=PARAMS,
        name="pack_rows",
    )(slc_images, chip_next, far_next, border)
    above, below = exchange(up, down, "row")
    left, right = pl.pallas_call(
        pack_columns_kernel,
        in_specs=[VMEM] * 6,
        out_specs=[VMEM, VMEM],
        out_shape=[shape((PADDED, LANES))] * 2,
        compiler_params=PARAMS,
        name="pack_columns",
    )(slc_images, chip_next, far_next, border, above, below)
    from_left, from_right = exchange(left, right, "col")

    mine = lax.dynamic_slice_in_dim(pair_list, 4 * myself, 4, axis=0)
    near = (mine // 2) == myself
    slots = jnp.where(near, 0, 2) + mine % 2
    table = jnp.concatenate([slots, look_sizes], axis=1)

    outs = [
        shape((4, 2, ROWS, COLS), F32),
        shape((4, ROWS, COLS), F32),
    ]
    interferogram, coherence = pl.pallas_call(
        near_kernel,
        grid=(3,),
        in_specs=[SMEM] + [VMEM] * 7,
        out_specs=[
            pl.BlockSpec((1, 2, ROWS, COLS), lambda i: (jnp.where(i == 0, 0, i + 1), 0, 0, 0)),
            pl.BlockSpec((1, ROWS, COLS), lambda i: (jnp.where(i == 0, 0, i + 1), 0, 0)),
        ],
        out_shape=outs,
        scratch_shapes=scratch(4),
        compiler_params=PARAMS,
        name="near_pairs",
    )(table, slc_images, chip_next, far_next, above, below, from_left, from_right)
    return pl.pallas_call(
        far_kernel,
        grid=(1,),
        in_specs=[SMEM] + [VMEM] * 7 + [pl.BlockSpec(memory_space=pl.ANY)] * 2,
        out_specs=[
            pl.BlockSpec((1, 2, ROWS, COLS), lambda i: (1, 0, 0, 0)),
            pl.BlockSpec((1, ROWS, COLS), lambda i: (1, 0, 0)),
        ],
        out_shape=outs,
        scratch_shapes=scratch(2),
        input_output_aliases={8: 0, 9: 1},
        compiler_params=PARAMS,
        name="far_pair",
    )(table, slc_images, border, inner, above, below, from_left, from_right, interferogram, coherence)


def solution(mesh):
    placed = (P("epoch", None, "row", "col"), P(), P("epoch", None))
    return jax.shard_map(
        body,
        mesh=mesh,
        in_specs=placed,
        out_specs=(P("epoch", None, "row", "col"), P("epoch", "row", "col")),
        check_vma=False,
    )
```

```python
import jax
import jax.numpy as jnp
from jax import lax
from jax.experimental import pallas as pl
from jax.experimental.pallas import tpu as pltpu
from jax.sharding import PartitionSpec as P

HALO = 8
LANES = 128
ROWS = 64
COLS = 1024
BLOCKS = COLS // LANES
PADDED = ROWS + 2 * HALO
F32 = jnp.float32
BF16 = jnp.bfloat16
VMEM_LIMIT = 48 * 1024 * 1024


def lane_iota(rows):
    return lax.broadcasted_iota(jnp.int32, (rows, LANES), 1)


def move_strip(values, source, target):
    return pltpu.roll(values, (target - source) % LANES, 1)


def put_strip(total, values, source, target):
    lane = lane_iota(values.shape[0])
    inside = (lane >= target) & (lane < target + HALO)
    return jnp.where(inside, move_strip(values, source, target), total)


def block(index):
    return slice(index * LANES, (index + 1) * LANES)


def far_lane(part, field, side):
    return HALO * (part * 4 + field * 2 + side)


def my_index(pairs, pair, column):
    return pairs[4 * lax.axis_index("epoch") + pair, column]


def asked(pairs):
    groups = lax.axis_size("epoch")
    myself = lax.axis_index("epoch")
    asker = lax.rem(myself + groups // 2, groups)
    return pairs[4 * asker + 1, 1] - 2 * myself


def select_kernel(pairs, images, selected):
    selected[...] = images[asked(pairs)]


def next_rows(one, other, k, field, rows, column):
    at = block(column)
    return one[k, field, rows, at].astype(F32) + other[k, field, rows, at].astype(F32)


def pack_rows_kernel(images, one, other, up, down):
    for acquisition in range(4):
        at = pl.ds(acquisition * 16, 16)
        for column in range(BLOCKS):
            for ref, rows, part in (
                (up, slice(0, 16), slice(0, HALO)),
                (down, slice(ROWS - 16, ROWS), slice(HALO, 16)),
            ):
                fields = []
                for field in range(2):
                    if acquisition < 2:
                        values = images[acquisition, field, rows, block(column)].astype(F32)
                    else:
                        values = next_rows(one, other, acquisition - 2, field, rows, column)
                    fields.append(values[part])
                ref[at, block(column)] = jnp.concatenate(fields, axis=0).astype(BF16)


def halo_rows(above, below, acquisition, field, column):
    at = pl.ds(acquisition * 16, 16)
    rows = slice(field * HALO, (field + 1) * HALO)
    return (
        above[at, block(column)].astype(F32)[rows],
        below[at, block(column)].astype(F32)[rows],
    )


def pack_columns_kernel(images, one, other, above, below, left, right):
    everything = slice(0, ROWS)
    for side, column, ref in ((0, 0, left), (1, BLOCKS - 1, right)):
        total = jnp.zeros((PADDED, LANES), F32)
        for acquisition in range(4):
            for field in range(2):
                before, after = halo_rows(above, below, acquisition, field, column)
                if acquisition < 2:
                    main = images[acquisition, field, :, block(column)].astype(F32)
                else:
                    main = next_rows(one, other, acquisition - 2, field, everything, column)
                total = put_strip(
                    total,
                    jnp.concatenate([before, main, after], axis=0),
                    side * (LANES - HALO),
                    HALO * (2 * acquisition + field),
                )
        ref[...] = total.astype(BF16)


PARTS = ((0, 32), (32, 32), (64, 16))


def pack_far_halo_kernel(pairs, above, below, from_left, from_right, halo):
    which = asked(pairs)
    at = pl.ds(pl.multiple_of(which * 16, 16), 16)
    for column in range(BLOCKS):
        rows = above[at, block(column)].astype(F32), below[at, block(column)].astype(F32)
        for field in range(2):
            part = slice(field * HALO, (field + 1) * HALO)
            both = jnp.concatenate([rows[0][part], rows[1][part]], axis=0)
            halo[pl.ds(column * 32 + field * 16, 16), :] = both.astype(BF16)
    total = jnp.zeros((32, LANES), F32)
    for side, ref in ((0, from_left), (1, from_right)):
        values = ref[...].astype(F32)
        values = jnp.where(which == 0, values, move_strip(values, 2 * HALO, 0))
        for field in range(2):
            for part, (begin, count) in enumerate(PARTS):
                rows = values[begin : begin + count]
                if count < 32:
                    rows = jnp.concatenate([rows, jnp.zeros((32 - count, LANES), F32)], axis=0)
                total = put_strip(total, rows, HALO * field, far_lane(part, field, side))
    halo[pl.ds(BLOCKS * 32, 32), :] = total.astype(BF16)


def halo_block(from_left, from_right, acquisition, field):
    source = HALO * (2 * acquisition + field)
    blank = jnp.zeros((PADDED, LANES), F32)
    after = put_strip(blank, from_right[...].astype(F32), source, 0)
    return put_strip(after, from_left[...].astype(F32), source, LANES - HALO)


def box_sums(reference, secondary, looks, products, sums, write):
    half_rows, half_cols = looks
    for column in range(BLOCKS + 1):
        at = block(column)
        a, b = reference(0, at), reference(1, at)
        c, d = secondary(0, at), secondary(1, at)
        fields = (a * c + b * d, b * c - a * d, a * a + b * b, c * c + d * d)
        for f, value in enumerate(fields):
            high = value.astype(BF16)
            products[f, :PADDED, at] = high
            products[f, PADDED:, at] = (value - high.astype(F32)).astype(BF16)
    inner = lax.broadcasted_iota(jnp.int32, (ROWS, 2 * PADDED), 0)
    outer = lax.broadcasted_iota(jnp.int32, (ROWS, 2 * PADDED), 1)
    outer = jnp.where(outer >= PADDED, outer - PADDED, outer)
    row_band = (jnp.abs(outer - HALO - inner) <= half_rows).astype(F32).astype(BF16)
    outer = lax.broadcasted_iota(jnp.int32, (4 * LANES, 2 * LANES), 0)
    inner = lax.broadcasted_iota(jnp.int32, (4 * LANES, 2 * LANES), 1)
    col_band = (jnp.abs(outer - LANES - inner) <= half_cols).astype(F32).astype(BF16)
    for f in range(4):
        by_rows = jnp.dot(row_band, products[f], preferred_element_type=F32)
        high = by_rows.astype(BF16)
        low = (by_rows - high.astype(F32)).astype(BF16)
        for part, value in ((0, high), (1, low)):
            at = slice((2 * f + part) * ROWS, (2 * f + part + 1) * ROWS)
            sums[at, LANES : LANES + COLS] = value[:, :COLS]
            sums[at, :LANES] = value[:, COLS:]
            sums[at, LANES + COLS :] = value[:, COLS:]
    window = ((2 * half_rows + 1) * (2 * half_cols + 1)).astype(F32)
    scale = 1.0 / jnp.full((ROWS, 2 * LANES), window, F32)
    for j in range(BLOCKS // 2):
        both = jnp.dot(
            sums[:, j * 256 : j * 256 + 512], col_band, preferred_element_type=F32
        )
        real, imag, power, other = (
            both[2 * f * ROWS : (2 * f + 1) * ROWS] + both[(2 * f + 1) * ROWS : (2 * f + 2) * ROWS]
            for f in range(4)
        )
        coherence = jnp.sqrt(real * real + imag * imag) / jnp.sqrt(power * other)
        write(slice(j * 256, (j + 1) * 256), real * scale, imag * scale, coherence)


def stage(target, slot, main, halos, edges):
    for field in range(2):
        for column in range(BLOCKS):
            before, after = halos(field, column)
            target[slot, field, :, block(column)] = jnp.concatenate(
                [before, main(field, column), after], axis=0
            )
        target[slot, field, :, block(BLOCKS)] = edges(field)


def stage_mine(target, slot, acquisition, images, above, below, from_left, from_right):
    stage(
        target,
        slot,
        lambda field, column: images[acquisition, field, :, block(column)].astype(F32),
        lambda field, column: halo_rows(above, below, acquisition, field, column),
        lambda field: halo_block(from_left, from_right, acquisition, field),
    )


def writer(interferogram, coherence):
    def write(at, real, imag, value):
        interferogram[0, 0, :, at] = real
        interferogram[0, 1, :, at] = imag
        coherence[0, :, at] = value

    return write


def near_kernel(
    pairs, looks, images, one, other, above, below, from_left, from_right,
    interferogram, coherence, staged, products, sums,
):
    step = pl.program_id(0)

    @pl.when(step == 0)
    def _():
        for acquisition in range(2):
            stage_mine(
                staged, acquisition, acquisition, images, above, below, from_left, from_right
            )
        for k in range(2):
            stage(
                staged,
                2 + k,
                lambda field, column, k=k: next_rows(one, other, k, field, slice(0, ROWS), column),
                lambda field, column, k=k: halo_rows(above, below, 2 + k, field, column),
                lambda field, k=k: halo_block(from_left, from_right, 2 + k, field),
            )

    pair = jnp.where(step == 0, 0, step + 1)
    first, second = my_index(pairs, pair, 0), my_index(pairs, pair, 1)
    begin = 2 * lax.axis_index("epoch")
    inside = (second >= begin) & (second < begin + 2)
    second = (second & 1) + jnp.where(inside, 0, 2)
    box_sums(
        lambda field, at: staged[first - begin, field, :, at],
        lambda field, at: staged[second, field, :, at],
        (looks[pair, 0], looks[pair, 1]),
        products,
        sums,
        writer(interferogram, coherence),
    )


def far_kernel(
    pairs, looks, images, main, halo, above, below, from_left, from_right, _, __,
    interferogram, coherence, staged, products, sums,
):
    first = my_index(pairs, 1, 0) - 2 * lax.axis_index("epoch")
    for acquisition in range(2):

        @pl.when(first == acquisition)
        def _(acquisition=acquisition):
            stage_mine(staged, 0, acquisition, images, above, below, from_left, from_right)

    strips = halo[pl.ds(BLOCKS * 32, 32), :].astype(F32)

    def halos(field, column):
        rows = halo[pl.ds(column * 32 + field * 16, 16), :].astype(F32)
        return rows[:HALO], rows[HALO:]

    def edges(field):
        blank = jnp.zeros((32, LANES), F32)
        rows = []
        for part, (_, count) in enumerate(PARTS):
            both = put_strip(blank, strips, far_lane(part, field, 1), 0)
            both = put_strip(both, strips, far_lane(part, field, 0), LANES - HALO)
            rows.append(both[:count])
        return jnp.concatenate(rows, axis=0)

    stage(staged, 1, lambda field, column: main[field, :, block(column)].astype(F32), halos, edges)
    box_sums(
        lambda field, at: staged[0, field, :, at],
        lambda field, at: staged[1, field, :, at],
        (looks[1, 0], looks[1, 1]),
        products,
        sums,
        writer(interferogram, coherence),
    )


VMEM = pl.BlockSpec(memory_space=pltpu.VMEM)
SMEM = pl.BlockSpec(memory_space=pltpu.SMEM)
PARAMS = pltpu.CompilerParams(vmem_limit_bytes=VMEM_LIMIT)


def shape(dims, dtype=BF16):
    return jax.ShapeDtypeStruct(dims, dtype)


def scratch(acquisitions):
    return [
        pltpu.VMEM((acquisitions, 2, PADDED, COLS + LANES), F32),
        pltpu.VMEM((4, 2 * PADDED, COLS + LANES), BF16),
        pltpu.VMEM((8 * ROWS, COLS + 2 * LANES), BF16),
    ]


def exchange(first, last, axis):
    peers = lax.axis_size(axis)
    up = [(i, i + 1) for i in range(peers - 1)]
    down = [(j, i) for i, j in up]
    return lax.ppermute(last, axis, up), lax.ppermute(first, axis, down)


def local(kernel, operands, results, name, scalars=0):
    return pl.pallas_call(
        kernel,
        in_specs=[SMEM] * scalars + [VMEM] * (len(operands) - scalars),
        out_specs=[VMEM] * len(results),
        out_shape=results,
        compiler_params=PARAMS,
        name=name,
    )(*operands)


def body(slc_images, pair_list, look_sizes):
    groups = lax.axis_size("epoch")
    swap = [(b, (b + groups // 2) % groups) for b in range(groups)]

    one = lax.ppermute(slc_images, "epoch", [(b + 1, b) for b in range(groups - 1)])
    (selected,) = local(
        select_kernel, (pair_list, slc_images), [shape((2, ROWS, COLS))], "select", 1
    )
    main = lax.ppermute(selected, "epoch", swap)
    other = lax.ppermute(slc_images, "epoch", [(groups - 2, groups - 1)])

    up, down = local(
        pack_rows_kernel, (slc_images, one, other), [shape((64, COLS))] * 2, "pack_rows"
    )
    above, below = exchange(up, down, "row")
    left, right = local(
        pack_columns_kernel,
        (slc_images, one, other, above, below),
        [shape((PADDED, LANES))] * 2,
        "pack_columns",
    )
    from_left, from_right = exchange(left, right, "col")
    edges = (above, below, from_left, from_right)
    (halo,) = local(
        pack_far_halo_kernel,
        (pair_list, *edges),
        [shape((BLOCKS * 32 + 32, LANES))],
        "pack_far_halo",
        1,
    )
    halo = lax.ppermute(halo, "epoch", swap)

    outs = [shape((4, 2, ROWS, COLS), F32), shape((4, ROWS, COLS), F32)]
    interferogram, coherence = pl.pallas_call(
        near_kernel,
        grid=(3,),
        in_specs=[SMEM] * 2 + [VMEM] * 7,
        out_specs=[
            pl.BlockSpec((1, 2, ROWS, COLS), lambda i: (jnp.where(i == 0, 0, i + 1), 0, 0, 0)),
            pl.BlockSpec((1, ROWS, COLS), lambda i: (jnp.where(i == 0, 0, i + 1), 0, 0)),
        ],
        out_shape=outs,
        scratch_shapes=scratch(4),
        compiler_params=PARAMS,
        name="near_pairs",
    )(pair_list, look_sizes, slc_images, one, other, *edges)
    return pl.pallas_call(
        far_kernel,
        grid=(1,),
        in_specs=[SMEM] * 2 + [VMEM] * 7 + [pl.BlockSpec(memory_space=pl.ANY)] * 2,
        out_specs=[
            pl.BlockSpec((1, 2, ROWS, COLS), lambda i: (1, 0, 0, 0)),
            pl.BlockSpec((1, ROWS, COLS), lambda i: (1, 0, 0)),
        ],
        out_shape=outs,
        scratch_shapes=scratch(2),
        input_output_aliases={9: 0, 10: 1},
        compiler_params=PARAMS,
        name="far_pair",
    )(pair_list, look_sizes, slc_images, main, halo, *edges, interferogram, coherence)


def solution(mesh):
    placed = (P("epoch", None, "row", "col"), P(), P("epoch", None))
    return jax.shard_map(
        body,
        mesh=mesh,
        in_specs=placed,
        out_specs=(P("epoch", None, "row", "col"), P("epoch", "row", "col")),
        check_vma=False,
    )
```

```python
import jax
import jax.numpy as jnp
from jax import lax
from jax.experimental import pallas as pl
from jax.experimental.pallas import tpu as pltpu
from jax.sharding import PartitionSpec as P

HALO = 8
LANES = 128
ROWS = 64
COLS = 1024
BLOCKS = COLS // LANES
PADDED = ROWS + 2 * HALO
F32 = jnp.float32
BF16 = jnp.bfloat16
WORK = 20_000_000_000
VMEM_LIMIT = 48 * 1024 * 1024


def lane_iota(rows):
    return lax.broadcasted_iota(jnp.int32, (rows, LANES), 1)


def move_strip(values, source, target):
    return pltpu.roll(values, (target - source) % LANES, 1)


def put_strip(total, values, source, target):
    lane = lane_iota(values.shape[0])
    inside = (lane >= target) & (lane < target + HALO)
    return jnp.where(inside, move_strip(values, source, target), total)


def block(index):
    return slice(index * LANES, (index + 1) * LANES)


def far_lane(part, field, side):
    return HALO * (part * 4 + field * 2 + side)


def my_index(pairs, pair, which):
    return pairs[which, 4 * lax.axis_index("epoch") + pair]


def asked(pairs):
    groups = lax.axis_size("epoch")
    myself = lax.axis_index("epoch")
    asker = lax.rem(myself + groups // 2, groups)
    return pairs[1, 4 * asker + 1] - 2 * myself


def split_kernel(pairs, images, border, own_up, own_down, own_columns, held, done):
    copies = [
        pltpu.make_async_copy(images.at[a, f], held.at[a, f], done.at[a, f])
        for a in range(2)
        for f in range(2)
    ]
    for copy in copies:
        copy.start()
    lead = asked(pairs)
    for copy in copies:
        copy.wait()
    strips = jnp.zeros((16, LANES), F32)
    for column in range(BLOCKS):
        for field in range(2):
            values = held[lead, field, :, block(column)].astype(F32)
            rows = jnp.concatenate([values[:HALO], values[ROWS - HALO :]], axis=0)
            border[pl.ds(column * 32 + field * 16, 16), :] = rows.astype(BF16)
            for side, at in ((0, 0), (1, BLOCKS - 1)):
                if column == at:
                    for part in range(3):
                        begin = HALO + 16 * part
                        strips = put_strip(
                            strips,
                            values[begin : begin + 16],
                            side * (LANES - HALO),
                            far_lane(part, field, side),
                        )
    border[pl.ds(BLOCKS * 32, 16), :] = strips.astype(BF16)
    for a in range(2):
        at = pl.ds(a * 16, 16)
        for column in range(BLOCKS):
            tops, bottoms = [], []
            for field in range(2):
                tops.append(held[a, field, :16, block(column)].astype(F32)[:HALO])
                bottoms.append(held[a, field, ROWS - 16 :, block(column)].astype(F32)[HALO:])
            own_up[at, block(column)] = jnp.concatenate(tops, axis=0).astype(BF16)
            own_down[at, block(column)] = jnp.concatenate(bottoms, axis=0).astype(BF16)
        for field in range(2):
            own_columns[2 * a + field, :, block(0)] = held[a, field, :, block(0)]
            own_columns[2 * a + field, :, block(1)] = held[a, field, :, block(BLOCKS - 1)]


def next_rows(one, other, k, field, rows, column):
    at = block(column)
    return one[k, field, rows, at].astype(F32) + other[k, field, rows, at].astype(F32)


def fields_of(a, b, c, d):
    return a * c + b * d, b * c - a * d, a * a + b * b, c * c + d * d


def put_split(target, f, at, value):
    count = value.shape[0]
    high = value.astype(BF16)
    target[f, :count, at] = high
    target[f, count : 2 * count, at] = (value - high.astype(F32)).astype(BF16)


def row_band(half_rows, count, row_of):
    inner = lax.broadcasted_iota(jnp.int32, (ROWS, 2 * count), 0)
    outer = lax.broadcasted_iota(jnp.int32, (ROWS, 2 * count), 1)
    outer = row_of(jnp.where(outer >= count, outer - count, outer))
    return (jnp.abs(outer - inner) <= half_rows).astype(F32).astype(BF16)


def border_row(k):
    return jnp.where(k < HALO, k - HALO, k + ROWS - HALO)


def wide_border_row(k):
    return jnp.where(k < 16, k - HALO, k + ROWS - 3 * HALO)


def row_sums(band, products):
    return jnp.dot(band, products, preferred_element_type=F32)


def pair_of(step):
    return jnp.where(step == 0, 0, step + 1)


def near_slots(pairs, pair):
    begin = 2 * lax.axis_index("epoch")
    second = my_index(pairs, pair, 1)
    inside = (second >= begin) & (second < begin + 2)
    return my_index(pairs, pair, 0) - begin, (second & 1) + jnp.where(inside, 0, 2)


def main_rows_kernel(pairs, looks, images, one, other, inner, partial, held, products):
    lead = asked(pairs)
    held[:2] = images[...]
    for column in range(BLOCKS):
        at = block(column)
        for field in range(2):
            values = images[lead, field, :, at].astype(F32)
            inner[field, :, at] = values[HALO : ROWS - HALO].astype(BF16)
            for k in range(2):
                values = next_rows(one, other, k, field, slice(0, ROWS), column)
                held[2 + k, field, :, at] = values.astype(BF16)

    def one_pair(step, carry):
        pair = pair_of(step)
        first, second = near_slots(pairs, pair)
        for column in range(BLOCKS):
            at = block(column)
            a, b = (held[first, field, :, at].astype(F32) for field in range(2))
            c, d = (held[second, field, :, at].astype(F32) for field in range(2))
            for f, value in enumerate(fields_of(a, b, c, d)):
                put_split(products, f, at, value)
        band = row_band(looks[0, pair], ROWS, lambda k: k)
        for f in range(4):
            partial[4 * step + f] = row_sums(band, products[f])
        return carry

    lax.fori_loop(0, 3, one_pair, 0)
    first = my_index(pairs, 1, 0) - 2 * lax.axis_index("epoch")
    for column in range(BLOCKS):
        at = block(column)
        a, b = (held[first, field, :, at].astype(F32) for field in range(2))
        put_split(products, 0, at, a * a + b * b)
    partial[12] = row_sums(row_band(looks[0, 1], ROWS, lambda k: k), products[0])


def pack_rows_kernel(own_up, own_down, one, other, border, up, down):
    up[:32, :] = own_up[...]
    down[:32, :] = own_down[...]
    for column in range(BLOCKS):
        at = block(column)
        for k in range(2):
            tops, bottoms = [], []
            for field in range(2):
                tops.append(next_rows(one, other, k, field, slice(0, 16), column)[:HALO])
                bottoms.append(
                    next_rows(one, other, k, field, slice(ROWS - 16, ROWS), column)[HALO:]
                )
            rows = pl.ds(32 + 16 * k, 16)
            up[rows, at] = jnp.concatenate(tops, axis=0).astype(BF16)
            down[rows, at] = jnp.concatenate(bottoms, axis=0).astype(BF16)
        real = border[pl.ds(column * 32, 16), :].astype(F32)
        imag = border[pl.ds(column * 32 + 16, 16), :].astype(F32)
        up[64:, at] = jnp.concatenate([real[:HALO], imag[:HALO]], axis=0).astype(BF16)
        down[64:, at] = jnp.concatenate([real[HALO:], imag[HALO:]], axis=0).astype(BF16)


def halo_rows(above, below, acquisition, field, column):
    at = pl.ds(acquisition * 16, 16)
    rows = slice(field * HALO, (field + 1) * HALO)
    return (
        above[at, block(column)].astype(F32)[rows],
        below[at, block(column)].astype(F32)[rows],
    )


def pack_columns_kernel(own_columns, one, other, border, above, below, left, right):
    strips = border[pl.ds(BLOCKS * 32, 16), :].astype(F32)
    for side, column, ref in ((0, 0, left), (1, BLOCKS - 1, right)):
        total = jnp.zeros((PADDED, LANES), F32)
        source = side * (LANES - HALO)
        for acquisition in range(5):
            for field in range(2):
                before, after = halo_rows(above, below, acquisition, field, column)
                if acquisition < 2:
                    main = own_columns[2 * acquisition + field, :, block(side)].astype(F32)
                elif acquisition < 4:
                    main = next_rows(one, other, acquisition - 2, field, slice(0, ROWS), column)
                else:
                    rows = border[pl.ds(column * 32 + field * 16, 16), :].astype(F32)
                    inner = [
                        move_strip(strips, far_lane(part, field, side), source)
                        for part in range(3)
                    ]
                    main = jnp.concatenate([rows[:HALO], *inner, rows[HALO:]], axis=0)
                values = jnp.concatenate([before, main, after], axis=0)
                total = put_strip(total, values, source, HALO * (2 * acquisition + field))
        ref[...] = total.astype(BF16)


def halo_block(from_left, from_right, acquisition, field):
    source = HALO * (2 * acquisition + field)
    blank = jnp.zeros((PADDED, LANES), F32)
    after = put_strip(blank, from_right[...].astype(F32), source, 0)
    return put_strip(after, from_left[...].astype(F32), source, LANES - HALO)


def column_sums(by_rows, half_cols, sums, count, write):
    for f in range(count):
        value, edge = by_rows(f)
        for part in range(2):
            rows = slice((2 * f + part) * ROWS, (2 * f + part + 1) * ROWS)
            high, high_edge = value.astype(BF16), edge.astype(BF16)
            sums[rows, LANES : LANES + COLS] = high
            sums[rows, :LANES] = high_edge
            sums[rows, LANES + COLS :] = high_edge
            value, edge = value - high.astype(F32), edge - high_edge.astype(F32)
    outer = lax.broadcasted_iota(jnp.int32, (4 * LANES, 2 * LANES), 0)
    inner = lax.broadcasted_iota(jnp.int32, (4 * LANES, 2 * LANES), 1)
    band = (jnp.abs(outer - LANES - inner) <= half_cols).astype(F32).astype(BF16)
    for j in range(BLOCKS // 2):
        both = jnp.dot(
            sums[: 2 * count * ROWS, j * 256 : j * 256 + 512], band, preferred_element_type=F32
        )
        write(
            j,
            [
                both[2 * f * ROWS : (2 * f + 1) * ROWS]
                + both[(2 * f + 1) * ROWS : (2 * f + 2) * ROWS]
                for f in range(count)
            ],
        )


def result_copies(pair, slot, j, held, interferogram, coherence, done):
    at = pl.ds(j * 256, 256)
    return (
        pltpu.make_async_copy(
            held.at[slot, pl.ds(0, 2), :, at],
            interferogram.at[pair, :, :, at],
            done.at[slot, j, 0],
        ),
        pltpu.make_async_copy(
            held.at[slot, 2, :, at], coherence.at[pair, :, at], done.at[slot, j, 1]
        ),
    )


def finish(real, imag, power, other, looks, pair, slot, j, results):
    held = results[0]
    window = ((2 * looks[0] + 1) * (2 * looks[1] + 1)).astype(F32)
    scale = 1.0 / jnp.full((8, 2 * LANES), window, F32)
    scale = jnp.concatenate([scale] * (ROWS // 8), axis=0)
    at = slice(j * 256, (j + 1) * 256)
    held[slot, 0, :, at] = real * scale
    held[slot, 1, :, at] = imag * scale
    held[slot, 2, :, at] = jnp.sqrt(real * real + imag * imag) / jnp.sqrt(power * other)
    for copy in result_copies(pair, slot, j, *results):
        copy.start()


def wait_for_results(pair, slot, results):
    for j in range(BLOCKS // 2):
        for copy in result_copies(pair, slot, j, *results):
            copy.wait()


def two_rows(upper, lower, acquisition, at):
    rows = pl.ds(pl.multiple_of(acquisition * 16, 16), 16)
    first, last = upper[rows, at].astype(F32), lower[rows, at].astype(F32)
    return (
        jnp.concatenate([first[:HALO], last[:HALO]], axis=0),
        jnp.concatenate([first[HALO:], last[HALO:]], axis=0),
    )


def near_kernel(
    pairs, looks, partial, own_up, own_down, border, above, below, from_left, from_right,
    interferogram, coherence, far_power, far_partial,
    halos, halo_products, edge_products, sums, held, done,
):
    for acquisition in range(5):
        for field in range(2):
            halos[acquisition, field] = halo_block(from_left, from_right, acquisition, field)
    results = held, interferogram, coherence, done
    everything = slice(0, LANES)

    def edge(slots, half_rows, fields):
        values = [halos[slot, field] for slot in slots for field in range(2)]
        band = row_band(half_rows, PADDED, lambda k: k - HALO)
        out = []
        for f, value in enumerate(fields(*values)):
            put_split(edge_products, f, everything, value)
            out.append(row_sums(band, edge_products[f]))
        return out

    def one_pair(step, carry):
        pair = pair_of(step)
        slots = near_slots(pairs, pair)
        half_rows, half_cols = looks[0, pair], looks[1, pair]
        for column in range(BLOCKS):
            at = block(column)
            values = [v for slot in slots for v in two_rows(above, below, slot, at)]
            for f, value in enumerate(fields_of(*values)):
                put_split(halo_products, f, at, value)
        band = row_band(half_rows, 16, border_row)
        edges = edge(slots, half_rows, fields_of)
        column_sums(
            lambda f: (
                partial[4 * step + f] + row_sums(band, halo_products[f, :32, :]),
                edges[f],
            ),
            half_cols,
            sums,
            4,
            lambda j, blocks: finish(
                *blocks, (half_rows, half_cols), pair, step, j, results
            ),
        )
        return carry

    lax.fori_loop(0, 3, one_pair, 0)

    first = my_index(pairs, 1, 0) - 2 * lax.axis_index("epoch")
    half_rows = looks[0, 1]

    def power(a, b):
        return (a * a + b * b,)

    for column in range(BLOCKS):
        at = block(column)
        put_split(halo_products, 0, at, power(*two_rows(above, below, first, at))[0])
    band = row_band(half_rows, 16, border_row)
    (edges,) = edge((first,), half_rows, power)

    def keep(j, blocks):
        far_power[:, j * 256 : (j + 1) * 256] = blocks[0]

    column_sums(
        lambda f: (partial[12] + row_sums(band, halo_products[0, :32, :]), edges),
        looks[1, 1],
        sums,
        1,
        keep,
    )

    def three(a, b, c, d):
        return a * c + b * d, b * c - a * d, c * c + d * d

    for column in range(BLOCKS):
        at = block(column)
        outside = two_rows(above, below, first, at)
        inside = two_rows(own_up, own_down, first, at)
        values = [
            jnp.concatenate([o[:HALO], i, o[HALO:]], axis=0)
            for o, i in zip(outside, inside, strict=True)
        ]
        outside = two_rows(above, below, 4, at)
        for field in range(2):
            inside = border[pl.ds(column * 32 + field * 16, 16), :].astype(F32)
            values.append(
                jnp.concatenate([outside[field][:HALO], inside, outside[field][HALO:]], axis=0)
            )
        for f, value in enumerate(three(*values)):
            put_split(halo_products, f, at, value)
    band = row_band(half_rows, 32, wide_border_row)
    edges = edge((first, 4), half_rows, three)
    for f in range(3):
        far_partial[f, :, :COLS] = row_sums(band, halo_products[f])
        far_partial[f, :, COLS:] = edges[f]
    for step, pair in enumerate((0, 2, 3)):
        wait_for_results(pair, step, results)


def far_kernel(
    pairs, looks, images, inner, far_power, far_partial, _, __,
    interferogram, coherence, products, sums, held, done,
):
    first = my_index(pairs, 1, 0) - 2 * lax.axis_index("epoch")
    sizes = looks[0, 1], looks[1, 1]
    results = held, interferogram, coherence, done
    for column in range(BLOCKS):
        at = block(column)
        a, b = (
            images[first, field, :, at].astype(F32)[HALO : ROWS - HALO] for field in range(2)
        )
        c, d = (inner[field, :, at].astype(F32) for field in range(2))
        for f, value in enumerate((a * c + b * d, b * c - a * d, c * c + d * d)):
            put_split(products, f, at, value)
    band = row_band(sizes[0], ROWS - 2 * HALO, lambda k: k + HALO)

    def write(j, blocks):
        real, imag, other = blocks
        power = far_power[:, j * 256 : (j + 1) * 256]
        finish(real, imag, power, other, sizes, 1, 0, j, results)

    column_sums(
        lambda f: (
            far_partial[f, :, :COLS] + row_sums(band, products[f]),
            far_partial[f, :, COLS:],
        ),
        sizes[1],
        sums,
        3,
        write,
    )
    wait_for_results(1, 0, results)


VMEM = pl.BlockSpec(memory_space=pltpu.VMEM)
SMEM = pl.BlockSpec(memory_space=pltpu.SMEM)
ANY = pl.BlockSpec(memory_space=pl.ANY)
PARAMS = pltpu.CompilerParams(vmem_limit_bytes=VMEM_LIMIT)


def shape(dims, dtype=BF16):
    return jax.ShapeDtypeStruct(dims, dtype)


def exchange(first, last, axis):
    peers = lax.axis_size(axis)
    up = [(i, i + 1) for i in range(peers - 1)]
    down = [(j, i) for i, j in up]
    return lax.ppermute(last, axis, up), lax.ppermute(first, axis, down)


def local(kernel, operands, places, results, name, kept=None, held=(), aliases=None, flops=0):
    return pl.pallas_call(
        kernel,
        in_specs=places,
        out_specs=kept or [VMEM] * len(results),
        out_shape=results,
        scratch_shapes=list(held),
        input_output_aliases=aliases or {},
        compiler_params=PARAMS,
        cost_estimate=pl.CostEstimate(flops=flops, bytes_accessed=0, transcendentals=0),
        name=name,
    )(*operands)


def body(slc_images, pair_list, look_sizes):
    groups = lax.axis_size("epoch")
    swap = [(b, (b + groups // 2) % groups) for b in range(groups)]
    pairs, looks = pair_list.T, look_sizes.T

    one = lax.ppermute(slc_images, "epoch", [(b + 1, b) for b in range(groups - 1)])
    border, own_up, own_down, own_columns, images = local(
        split_kernel,
        (pairs, slc_images),
        [SMEM, ANY],
        [
            shape((BLOCKS * 32 + 16, LANES)),
            shape((32, COLS)),
            shape((32, COLS)),
            shape((4, ROWS, 2 * LANES)),
            shape((2, 2, ROWS, COLS)),
        ],
        "split",
        held=[pltpu.SemaphoreType.DMA((2, 2))],
    )
    border = lax.ppermute(border, "epoch", swap)
    other = lax.ppermute(images, "epoch", [(groups - 2, groups - 1)])
    inner, partial = local(
        main_rows_kernel,
        (pairs, looks, images, one, other),
        [SMEM] * 2 + [VMEM] * 3,
        [shape((2, ROWS - 2 * HALO, COLS)), shape((13, ROWS, COLS), F32)],
        "main_rows",
        held=[
            pltpu.VMEM((4, 2, ROWS, COLS), BF16),
            pltpu.VMEM((4, 2 * ROWS, COLS), BF16),
        ],
        flops=WORK,
    )
    inner = lax.ppermute(inner, "epoch", swap)

    up, down = local(
        pack_rows_kernel,
        (own_up, own_down, one, other, border),
        [VMEM] * 5,
        [shape((80, COLS))] * 2,
        "pack_rows",
    )
    above, below = exchange(up, down, "row")
    left, right = local(
        pack_columns_kernel,
        (own_columns, one, other, border, above, below),
        [VMEM] * 6,
        [shape((PADDED, LANES))] * 2,
        "pack_columns",
    )
    edges = (above, below, *exchange(left, right, "col"))

    outs = [shape((4, 2, ROWS, COLS), F32), shape((4, ROWS, COLS), F32)]
    interferogram, coherence, power, rest = local(
        near_kernel,
        (pairs, looks, partial, own_up, own_down, border, *edges),
        [SMEM] * 2 + [VMEM] * 8,
        [*outs, shape((ROWS, COLS), F32), shape((3, ROWS, COLS + LANES), F32)],
        "near_pairs",
        kept=[ANY, ANY, VMEM, VMEM],
        held=[
            pltpu.VMEM((5, 2, PADDED, LANES), F32),
            pltpu.VMEM((4, 64, COLS), BF16),
            pltpu.VMEM((4, 2 * PADDED, LANES), BF16),
            pltpu.VMEM((8 * ROWS, COLS + 2 * LANES), BF16),
            pltpu.VMEM((3, 3, ROWS, COLS), F32),
            pltpu.SemaphoreType.DMA((3, BLOCKS // 2, 2)),
        ],
    )
    return local(
        far_kernel,
        (pairs, looks, images, inner, power, rest, interferogram, coherence),
        [SMEM] * 2 + [VMEM] * 4 + [ANY] * 2,
        outs,
        "far_pair",
        kept=[ANY, ANY],
        held=[
            pltpu.VMEM((3, 2 * (ROWS - 2 * HALO), COLS), BF16),
            pltpu.VMEM((6 * ROWS, COLS + 2 * LANES), BF16),
            pltpu.VMEM((1, 3, ROWS, COLS), F32),
            pltpu.SemaphoreType.DMA((1, BLOCKS // 2, 2)),
        ],
        aliases={6: 0, 7: 1},
    )


def solution(mesh):
    placed = (P("epoch", None, "row", "col"), P(), P("epoch", None))
    return jax.shard_map(
        body,
        mesh=mesh,
        in_specs=placed,
        out_specs=(P("epoch", None, "row", "col"), P("epoch", "row", "col")),
        check_vma=False,
    )
```

```python
import jax
import jax.numpy as jnp
from jax import lax
from jax.experimental import pallas as pl
from jax.experimental.pallas import tpu as pltpu
from jax.sharding import PartitionSpec as P

HALO = 8
LANES = 128
ROWS = 64
COLS = 1024
BLOCKS = COLS // LANES
PADDED = ROWS + 2 * HALO
F32 = jnp.float32
BF16 = jnp.bfloat16
WORK = 20_000_000_000
LITTLE = 100_000_000
VMEM_LIMIT = 24 * 1024 * 1024


def lane_iota(rows):
    return lax.broadcasted_iota(jnp.int32, (rows, LANES), 1)


def move_strip(values, source, target):
    return pltpu.roll(values, (target - source) % LANES, 1)


def put_strip(total, values, source, target):
    lane = lane_iota(values.shape[0])
    inside = (lane >= target) & (lane < target + HALO)
    return jnp.where(inside, move_strip(values, source, target), total)


def block(index):
    return slice(index * LANES, (index + 1) * LANES)


def far_lane(part, field, side):
    return HALO * (part * 4 + field * 2 + side)


def my_index(pairs, pair, which):
    return pairs[which, 4 * lax.axis_index("epoch") + pair]


def look(pairs, pair, which):
    return pairs[which, 4 * lax.axis_size("epoch") + pair]


def is_last():
    return lax.axis_index("epoch") == lax.axis_size("epoch") - 1


def asked(pairs):
    groups = lax.axis_size("epoch")
    myself = lax.axis_index("epoch")
    asker = lax.rem(myself + groups // 2, groups)
    return pairs[1, 4 * asker + 1] - 2 * myself


def split_kernel(pairs, images, border, kept):
    lead = asked(pairs)
    kept[...] = images[...]
    strips = jnp.zeros((16, LANES), F32)
    for column in range(BLOCKS):
        for field in range(2):
            first = images[lead, field, :16, block(column)].astype(F32)
            last = images[lead, field, ROWS - 16 :, block(column)].astype(F32)
            rows = jnp.concatenate([first[:HALO], last[HALO:]], axis=0)
            border[pl.ds(column * 32 + field * 16, 16), :] = rows.astype(BF16)
            for side, at in ((0, 0), (1, BLOCKS - 1)):
                if column == at:
                    values = images[lead, field, :, block(column)].astype(F32)
                    for part in range(3):
                        begin = HALO + 16 * part
                        strips = put_strip(
                            strips,
                            values[begin : begin + 16],
                            side * (LANES - HALO),
                            far_lane(part, field, side),
                        )
    border[pl.ds(BLOCKS * 32, 16), :] = strips.astype(BF16)


def next_rows(one, other, k, field, rows, column):
    at = block(column)
    return one[k, field, rows, at].astype(F32) + other[k, field, rows, at].astype(F32)


def fields_of(a, b, c, d):
    return a * c + b * d, b * c - a * d, a * a + b * b, c * c + d * d


def put_split(target, f, at, value):
    count = value.shape[0]
    high = value.astype(BF16)
    target[f, :count, at] = high
    target[f, count : 2 * count, at] = (value - high.astype(F32)).astype(BF16)


def row_band(half_rows, count, row_of):
    inner = lax.broadcasted_iota(jnp.int32, (ROWS, 2 * count), 0)
    outer = lax.broadcasted_iota(jnp.int32, (ROWS, 2 * count), 1)
    outer = row_of(jnp.where(outer >= count, outer - count, outer))
    return (jnp.abs(outer - inner) <= half_rows).astype(F32).astype(BF16)


def border_row(k):
    return jnp.where(k < HALO, k - HALO, k + ROWS - HALO)


def wide_border_row(k):
    return jnp.where(k < 16, k - HALO, k + ROWS - 3 * HALO)


def row_sums(band, products):
    return jnp.dot(band, products, preferred_element_type=F32)


def near_slots(pairs, pair):
    begin = 2 * lax.axis_index("epoch")
    second = my_index(pairs, pair, 1)
    inside = (second >= begin) & (second < begin + 2)
    return my_index(pairs, pair, 0) - begin, (second & 1) + jnp.where(inside, 0, 2)


def column_band(half_cols):
    outer = lax.broadcasted_iota(jnp.int32, (4 * LANES, 2 * LANES), 0)
    inner = lax.broadcasted_iota(jnp.int32, (4 * LANES, 2 * LANES), 1)
    return (jnp.abs(outer - LANES - inner) <= half_cols).astype(F32).astype(BF16)


def own_kernel(
    pairs, images, inner, powers, own_up, own_down, own_columns, bands, products
):
    lead = asked(pairs)
    for column in range(BLOCKS):
        at = block(column)
        for field in range(2):
            values = images[lead, field, :, at].astype(F32)
            inner[field, :, at] = values[HALO : ROWS - HALO].astype(BF16)
    for a in range(2):
        rows = pl.ds(a * 16, 16)
        for column in range(BLOCKS):
            at = block(column)
            tops, bottoms = [], []
            for field in range(2):
                tops.append(images[a, field, :16, at].astype(F32)[:HALO])
                bottoms.append(images[a, field, ROWS - 16 :, at].astype(F32)[HALO:])
            own_up[rows, at] = jnp.concatenate(tops, axis=0).astype(BF16)
            own_down[rows, at] = jnp.concatenate(bottoms, axis=0).astype(BF16)
        for field in range(2):
            own_columns[2 * a + field, :, block(0)] = images[a, field, :, block(0)]
            own_columns[2 * a + field, :, block(1)] = images[a, field, :, block(BLOCKS - 1)]
    for pair in range(4):
        first = my_index(pairs, pair, 0) - 2 * lax.axis_index("epoch")
        for column in range(BLOCKS):
            at = block(column)
            a, b = (images[first, field, :, at].astype(F32) for field in range(2))
            put_split(products, pair, at, a * a + b * b)
        band = row_band(look(pairs, pair, 0), ROWS, lambda k: k)
        powers[pair] = row_sums(band, products[pair])
        band = column_band(look(pairs, pair, 1))
        bands[pair, : 4 * LANES, :] = band
        bands[pair, 4 * LANES :, :] = band


def far_fields(a, b, c, d):
    return a * c + b * d, b * c - a * d, c * c + d * d


def near_rows_kernel(pairs, images, one, other, partial, held, products):
    held[:2] = images[...]
    for column in range(BLOCKS):
        at = block(column)
        for k in range(2):
            for field in range(2):
                values = next_rows(one, other, k, field, slice(0, ROWS), column)
                held[2 + k, field, :, at] = values.astype(BF16)

    def one_pair(step, carry):
        pair = jnp.where(step == 0, 0, step + 1)
        first, second = near_slots(pairs, pair)
        for column in range(BLOCKS):
            at = block(column)
            a, b = (held[first, field, :, at].astype(F32) for field in range(2))
            c, d = (held[second, field, :, at].astype(F32) for field in range(2))
            for f, value in enumerate(far_fields(a, b, c, d)):
                put_split(products, f, at, value)
        band = row_band(look(pairs, pair, 0), ROWS, lambda k: k)
        for f in range(3):
            partial[3 * step + f] = row_sums(band, products[f])
        return carry

    lax.fori_loop(0, 3, one_pair, 0)


def pack_rows_kernel(own_up, own_down, one, other, border, _, up, down):
    up[:32, :] = own_up[...]
    down[:32, :] = own_down[...]
    for column in range(BLOCKS):
        at = block(column)
        for k in range(2):
            tops, bottoms = [], []
            for field in range(2):
                tops.append(next_rows(one, other, k, field, slice(0, 16), column)[:HALO])
                bottoms.append(
                    next_rows(one, other, k, field, slice(ROWS - 16, ROWS), column)[HALO:]
                )
            rows = pl.ds(32 + 16 * k, 16)
            up[rows, at] = jnp.concatenate(tops, axis=0).astype(BF16)
            down[rows, at] = jnp.concatenate(bottoms, axis=0).astype(BF16)
        real = border[pl.ds(column * 32, 16), :].astype(F32)
        imag = border[pl.ds(column * 32 + 16, 16), :].astype(F32)
        up[64:, at] = jnp.concatenate([real[:HALO], imag[:HALO]], axis=0).astype(BF16)
        down[64:, at] = jnp.concatenate([real[HALO:], imag[HALO:]], axis=0).astype(BF16)


def halo_rows(above, below, acquisition, field, column):
    at = pl.ds(acquisition * 16, 16)
    rows = slice(field * HALO, (field + 1) * HALO)
    return (
        above[at, block(column)].astype(F32)[rows],
        below[at, block(column)].astype(F32)[rows],
    )


def pack_columns_kernel(own_columns, one, other, border, above, below, _, left, right):
    strips = border[pl.ds(BLOCKS * 32, 16), :].astype(F32)
    for side, column, ref in ((0, 0, left), (1, BLOCKS - 1, right)):
        total = jnp.zeros((PADDED, LANES), F32)
        source = side * (LANES - HALO)
        for acquisition in range(5):
            for field in range(2):
                before, after = halo_rows(above, below, acquisition, field, column)
                if acquisition < 2:
                    main = own_columns[2 * acquisition + field, :, block(side)].astype(F32)
                elif acquisition < 4:
                    main = next_rows(one, other, acquisition - 2, field, slice(0, ROWS), column)
                else:
                    rows = border[pl.ds(column * 32 + field * 16, 16), :].astype(F32)
                    inner = [
                        move_strip(strips, far_lane(part, field, side), source)
                        for part in range(3)
                    ]
                    main = jnp.concatenate([rows[:HALO], *inner, rows[HALO:]], axis=0)
                values = jnp.concatenate([before, main, after], axis=0)
                total = put_strip(total, values, source, HALO * (2 * acquisition + field))
        ref[...] = total.astype(BF16)


def halo_block(from_left, from_right, acquisition, field):
    source = HALO * (2 * acquisition + field)
    blank = jnp.zeros((PADDED, LANES), F32)
    after = put_strip(blank, from_right[...].astype(F32), source, 0)
    return put_strip(after, from_left[...].astype(F32), source, LANES - HALO)


def column_sums(j, band, rows, edges):
    begin, end = max(j * 256 - LANES, 0), min(j * 256 + 3 * LANES, COLS)
    parts = []
    for term in range(2):
        if j == 0:
            parts.append(edges(term))
        parts.append(rows(term, slice(begin, end)))
        if j == BLOCKS // 2 - 1:
            parts.append(edges(term))
    both = row_sums(jnp.concatenate(parts, axis=1), band)
    return [both[f : f + ROWS] for f in range(0, both.shape[0], ROWS)]


def put_terms(target, f, value, columns=slice(None)):
    high = value.astype(BF16)
    at = pl.ds(f * ROWS, ROWS)
    target[0, at, columns] = high
    target[1, at, columns] = (value - high.astype(F32)).astype(BF16)


def result_copies(pair, slot, j, held, interferogram, coherence, done):
    at = pl.ds(j * 256, 256)
    return (
        pltpu.make_async_copy(
            held.at[slot, pl.ds(0, 2), :, at],
            interferogram.at[pair, :, :, at],
            done.at[slot, j, 0],
        ),
        pltpu.make_async_copy(
            held.at[slot, 2, :, at], coherence.at[pair, :, at], done.at[slot, j, 1]
        ),
    )


def finish(real, imag, power, other, pairs, pair, slot, j, results):
    held = results[0]
    window = ((2 * look(pairs, pair, 0) + 1) * (2 * look(pairs, pair, 1) + 1)).astype(F32)
    scale = 1.0 / jnp.full((8, 2 * LANES), window, F32)
    scale = jnp.concatenate([scale] * (ROWS // 8), axis=0)
    at = slice(j * 256, (j + 1) * 256)
    held[slot, 0, :, at] = real * scale
    held[slot, 1, :, at] = imag * scale
    held[slot, 2, :, at] = jnp.sqrt(real * real + imag * imag) / jnp.sqrt(power * other)
    for copy in result_copies(pair, slot, j, *results):
        copy.start()


def wait_for_results(pair, slot, results):
    for j in range(BLOCKS // 2):
        for copy in result_copies(pair, slot, j, *results):
            copy.wait()


def two_rows(upper, lower, acquisition, at):
    rows = pl.ds(pl.multiple_of(acquisition * 16, 16), 16)
    first, last = upper[rows, at].astype(F32), lower[rows, at].astype(F32)
    return (
        jnp.concatenate([first[:HALO], last[:HALO]], axis=0),
        jnp.concatenate([first[HALO:], last[HALO:]], axis=0),
    )


def power_of(a, b):
    return (a * a + b * b,)


def halo_rows_kernel(
    pairs, powers, partial, own_up, own_down, border, above, below, terms, far_partial, products
):
    def add(slots, half_rows, fields, place, main):
        for column in range(BLOCKS):
            at = block(column)
            values = [v for slot in slots for v in two_rows(above, below, slot, at)]
            for f, value in enumerate(fields(*values)):
                put_split(products, f, at, value)
        band = row_band(half_rows, 16, border_row)
        for f, value in enumerate(main):
            put_terms(terms, place + f, value() + row_sums(band, products[f, :32, :]))

    def one_pair(step, carry):
        pair = jnp.where(step == 0, 0, step + 1)
        main = (
            lambda: partial[3 * step],
            lambda: partial[3 * step + 1],
            lambda: powers[pair],
            lambda: partial[3 * step + 2],
        )
        add(near_slots(pairs, pair), look(pairs, pair, 0), fields_of, 4 * step, main)
        return carry

    lax.fori_loop(0, 3, one_pair, 0)
    first = my_index(pairs, 1, 0) - 2 * lax.axis_index("epoch")
    half_rows = look(pairs, 1, 0)
    add((first,), half_rows, power_of, 12, (lambda: powers[1],))
    for column in range(BLOCKS):
        at = block(column)
        outside = two_rows(above, below, first, at)
        inside = two_rows(own_up, own_down, first, at)
        values = [
            jnp.concatenate([o[:HALO], i, o[HALO:]], axis=0)
            for o, i in zip(outside, inside, strict=True)
        ]
        outside = two_rows(above, below, 4, at)
        for field in range(2):
            inside = border[pl.ds(column * 32 + field * 16, 16), :].astype(F32)
            values.append(
                jnp.concatenate([outside[field][:HALO], inside, outside[field][HALO:]], axis=0)
            )
        for f, value in enumerate(far_fields(*values)):
            put_split(products, f, at, value)
    band = row_band(half_rows, 32, wide_border_row)
    for f in range(3):
        far_partial[f] = row_sums(band, products[f])


def near_kernel(
    pairs, bands, terms, from_left, from_right,
    interferogram, coherence, far_power, far_edges,
    halos, products, edges, held, done,
):
    for acquisition in range(5):
        for field in range(2):
            halos[acquisition, field] = halo_block(from_left, from_right, acquisition, field)
    results = held, interferogram, coherence, done
    everything = slice(0, LANES)

    def edge(target, slots, half_rows, fields):
        values = [halos[slot, field] for slot in slots for field in range(2)]
        band = row_band(half_rows, PADDED, lambda k: k - HALO)
        for f, value in enumerate(fields(*values)):
            put_split(products, f, everything, value)
            put_terms(target, f, row_sums(band, products[f]))

    def one_pair(step, carry):
        pair = jnp.where(step == 0, 0, step + 1)
        edge(edges, near_slots(pairs, pair), look(pairs, pair, 0), fields_of)
        at = pl.ds(pl.multiple_of(step * 4 * ROWS, 4 * ROWS), 4 * ROWS)
        for j in range(BLOCKS // 2):
            blocks = column_sums(
                j, bands[pair], lambda term, columns: terms[term, at, columns], lambda term: edges[term]
            )
            finish(*blocks, pairs, pair, step, j, results)
        return carry

    lax.fori_loop(0, 3, one_pair, 0)

    first = my_index(pairs, 1, 0) - 2 * lax.axis_index("epoch")
    edge(edges, (first,), look(pairs, 1, 0), power_of)
    for j in range(BLOCKS // 2):
        (far_power[:, j * 256 : (j + 1) * 256],) = column_sums(
            j,
            bands[1],
            lambda term, columns: terms[term, 12 * ROWS :, columns],
            lambda term: edges[term, :ROWS, :],
        )
    edge(far_edges, (first, 4), look(pairs, 1, 0), far_fields)
    for step, pair in enumerate((0, 2, 3)):
        wait_for_results(pair, step, results)


def far_kernel(
    pairs, bands, images, inner, far_power, far_partial, far_edges, _, __,
    interferogram, coherence, products, terms, held, done,
):
    first = my_index(pairs, 1, 0) - 2 * lax.axis_index("epoch")
    results = held, interferogram, coherence, done
    band = row_band(look(pairs, 1, 0), ROWS - 2 * HALO, lambda k: k + HALO)

    def rows(j):
        for column in (2 * j, 2 * j + 1):
            at = block(column)
            a, b = (
                images[first, field, :, at].astype(F32)[HALO : ROWS - HALO] for field in range(2)
            )
            c, d = (inner[field, :, at].astype(F32) for field in range(2))
            for f, value in enumerate(far_fields(a, b, c, d)):
                put_split(products, f, at, value)
        at = slice(j * 256, (j + 1) * 256)
        for f in range(3):
            put_terms(terms, f, far_partial[f, :, at] + row_sums(band, products[f, :, at]), at)

    def columns(j):
        real, imag, other = column_sums(
            j, bands[1], lambda term, at: terms[term, :, at], lambda term: far_edges[term]
        )
        power = far_power[:, j * 256 : (j + 1) * 256]
        finish(real, imag, power, other, pairs, 1, 0, j, results)

    rows(0)
    for j in range(1, BLOCKS // 2):
        rows(j)
        columns(j - 1)
    columns(BLOCKS // 2 - 1)
    wait_for_results(1, 0, results)


VMEM = pl.BlockSpec(memory_space=pltpu.VMEM)
SMEM = pl.BlockSpec(memory_space=pltpu.SMEM)
ANY = pl.BlockSpec(memory_space=pl.ANY)
PARAMS = pltpu.CompilerParams(vmem_limit_bytes=VMEM_LIMIT)


def shape(dims, dtype=BF16):
    return jax.ShapeDtypeStruct(dims, dtype)


def exchange(first, last, axis):
    peers = lax.axis_size(axis)
    up = [(i, i + 1) for i in range(peers - 1)]
    down = [(j, i) for i, j in up]
    return lax.ppermute(last, axis, up), lax.ppermute(first, axis, down)


def local(kernel, operands, places, results, name, kept=None, held=(), aliases=None, flops=0):
    return pl.pallas_call(
        kernel,
        in_specs=places,
        out_specs=kept or [VMEM] * len(results),
        out_shape=results,
        scratch_shapes=list(held),
        input_output_aliases=aliases or {},
        compiler_params=PARAMS,
        cost_estimate=pl.CostEstimate(flops=flops, bytes_accessed=0, transcendentals=0),
        name=name,
    )(*operands)


def body(slc_images, pair_list, look_sizes):
    groups = lax.axis_size("epoch")
    swap = [(b, (b + groups // 2) % groups) for b in range(groups)]
    table = jnp.concatenate([pair_list.T, look_sizes.T], axis=1)

    one = lax.ppermute(slc_images, "epoch", [(b + 1, b) for b in range(groups - 1)])
    border, images = local(
        split_kernel,
        (table, slc_images),
        [SMEM, VMEM],
        [shape((BLOCKS * 32 + 16, LANES)), shape((2, 2, ROWS, COLS))],
        "split",
    )
    border = lax.ppermute(border, "epoch", swap)
    inner, powers, own_up, own_down, own_columns, bands = local(
        own_kernel,
        (table, images),
        [SMEM, VMEM],
        [
            shape((2, ROWS - 2 * HALO, COLS)),
            shape((4, ROWS, COLS), F32),
            shape((32, COLS)),
            shape((32, COLS)),
            shape((4, ROWS, 2 * LANES)),
            shape((4, 8 * LANES, 2 * LANES)),
        ],
        "own",
        held=[pltpu.VMEM((4, 2 * ROWS, COLS), BF16)],
        flops=WORK,
    )
    inner = lax.ppermute(inner, "epoch", swap)
    other = lax.ppermute(images, "epoch", [(groups - 2, groups - 1)])

    up, down = local(
        pack_rows_kernel,
        (own_up, own_down, one, other, border, powers),
        [VMEM] * 6,
        [shape((80, COLS))] * 2,
        "pack_rows",
    )
    above, below = exchange(up, down, "row")
    (partial,) = local(
        near_rows_kernel,
        (table, images, one, other),
        [SMEM] + [VMEM] * 3,
        [shape((9, ROWS, COLS), F32)],
        "near_rows",
        held=[
            pltpu.VMEM((4, 2, ROWS, COLS), BF16),
            pltpu.VMEM((3, 2 * ROWS, COLS), BF16),
        ],
        flops=LITTLE,
    )
    left, right = local(
        pack_columns_kernel,
        (own_columns, one, other, border, above, below, partial),
        [VMEM] * 7,
        [shape((PADDED, LANES))] * 2,
        "pack_columns",
    )
    from_left, from_right = exchange(left, right, "col")
    terms, rest = local(
        halo_rows_kernel,
        (table, powers, partial, own_up, own_down, border, above, below),
        [SMEM] + [VMEM] * 7,
        [shape((2, 13 * ROWS, COLS)), shape((3, ROWS, COLS), F32)],
        "halo_rows",
        held=[pltpu.VMEM((4, 64, COLS), BF16)],
        flops=LITTLE,
    )

    outs = [shape((4, 2, ROWS, COLS), F32), shape((4, ROWS, COLS), F32)]
    interferogram, coherence, power, edges = local(
        near_kernel,
        (table, bands, terms, from_left, from_right),
        [SMEM] + [VMEM] * 4,
        [*outs, shape((ROWS, COLS), F32), shape((2, 3 * ROWS, LANES))],
        "near_pairs",
        kept=[ANY, ANY, VMEM, VMEM],
        held=[
            pltpu.VMEM((5, 2, PADDED, LANES), F32),
            pltpu.VMEM((4, 2 * PADDED, LANES), BF16),
            pltpu.VMEM((2, 4 * ROWS, LANES), BF16),
            pltpu.VMEM((3, 3, ROWS, COLS), F32),
            pltpu.SemaphoreType.DMA((3, BLOCKS // 2, 2)),
        ],
    )
    return local(
        far_kernel,
        (table, bands, images, inner, power, rest, edges, interferogram, coherence),
        [SMEM] + [VMEM] * 6 + [ANY] * 2,
        outs,
        "far_pair",
        kept=[ANY, ANY],
        held=[
            pltpu.VMEM((3, 2 * (ROWS - 2 * HALO), COLS), BF16),
            pltpu.VMEM((2, 3 * ROWS, COLS), BF16),
            pltpu.VMEM((1, 3, ROWS, COLS), F32),
            pltpu.SemaphoreType.DMA((1, BLOCKS // 2, 2)),
        ],
        aliases={7: 0, 8: 1},
    )


def solution(mesh):
    placed = (P("epoch", None, "row", "col"), P(), P("epoch", None))
    return jax.shard_map(
        body,
        mesh=mesh,
        in_specs=placed,
        out_specs=(P("epoch", None, "row", "col"), P("epoch", "row", "col")),
        check_vma=False,
    )
```

```python
import jax
import jax.numpy as jnp
from jax import lax
from jax.experimental import pallas as pl
from jax.experimental.pallas import tpu as pltpu
from jax.sharding import PartitionSpec as P

HALO = 8
LANES = 128
ROWS = 64
COLS = 1024
BLOCKS = COLS // LANES
PADDED = ROWS + 2 * HALO
F32 = jnp.float32
BF16 = jnp.bfloat16
WORK = 20_000_000_000
LITTLE = 100_000_000
VMEM_LIMIT = 24 * 1024 * 1024


def lane_iota(rows):
    return lax.broadcasted_iota(jnp.int32, (rows, LANES), 1)


def move_strip(values, source, target):
    return pltpu.roll(values, (target - source) % LANES, 1)


def put_strip(total, values, source, target):
    lane = lane_iota(values.shape[0])
    inside = (lane >= target) & (lane < target + HALO)
    return jnp.where(inside, move_strip(values, source, target), total)


def block(index):
    return slice(index * LANES, (index + 1) * LANES)


def far_lane(part, field, side):
    return HALO * (part * 4 + field * 2 + side)


def my_index(pairs, pair, which):
    return pairs[which, 4 * lax.axis_index("epoch") + pair]


def look(pairs, pair, which):
    return pairs[which, 4 * lax.axis_size("epoch") + pair]


def is_last():
    return lax.axis_index("epoch") == lax.axis_size("epoch") - 1


def asked(pairs):
    groups = lax.axis_size("epoch")
    myself = lax.axis_index("epoch")
    asker = lax.rem(myself + groups // 2, groups)
    return pairs[1, 4 * asker + 1] - 2 * myself


def split_kernel(pairs, images, border, kept):
    kept[...] = images[...]
    lead = asked(pairs)

    def chosen(field, rows, column):
        return images[lead, field, rows, block(column)].astype(F32)

    strips = jnp.zeros((16, LANES), F32)
    for column in range(BLOCKS):
        for field in range(2):
            first = chosen(field, slice(0, 16), column)
            last = chosen(field, slice(ROWS - 16, ROWS), column)
            rows = jnp.concatenate([first[:HALO], last[HALO:]], axis=0)
            border[pl.ds(column * 32 + field * 16, 16), :] = rows.astype(BF16)
            for side, at in ((0, 0), (1, BLOCKS - 1)):
                if column == at:
                    values = chosen(field, slice(0, ROWS), column)
                    for part in range(3):
                        begin = HALO + 16 * part
                        strips = put_strip(
                            strips,
                            values[begin : begin + 16],
                            side * (LANES - HALO),
                            far_lane(part, field, side),
                        )
    border[pl.ds(BLOCKS * 32, 16), :] = strips.astype(BF16)


def next_rows(one, other, k, field, rows, column):
    at = block(column)
    return one[k, field, rows, at].astype(F32) + other[k, field, rows, at].astype(F32)


def fields_of(a, b, c, d):
    return a * c + b * d, b * c - a * d, a * a + b * b, c * c + d * d


def put_split(target, f, at, value):
    count = value.shape[0]
    high = value.astype(BF16)
    target[f, :count, at] = high
    target[f, count : 2 * count, at] = (value - high.astype(F32)).astype(BF16)


def row_band(half_rows, count, row_of):
    inner = lax.broadcasted_iota(jnp.int32, (ROWS, 2 * count), 0)
    outer = lax.broadcasted_iota(jnp.int32, (ROWS, 2 * count), 1)
    outer = row_of(jnp.where(outer >= count, outer - count, outer))
    return (jnp.abs(outer - inner) <= half_rows).astype(F32).astype(BF16)


def border_row(k):
    return jnp.where(k < HALO, k - HALO, k + ROWS - HALO)


def wide_border_row(k):
    return jnp.where(k < 16, k - HALO, k + ROWS - 3 * HALO)


def row_sums(band, products):
    return jnp.dot(band, products, preferred_element_type=F32)


def column_band(half_cols):
    outer = lax.broadcasted_iota(jnp.int32, (4 * LANES, 2 * LANES), 0)
    inner = lax.broadcasted_iota(jnp.int32, (4 * LANES, 2 * LANES), 1)
    return (jnp.abs(outer - LANES - inner) <= half_cols).astype(F32).astype(BF16)


def near_slots(pairs, pair):
    begin = 2 * lax.axis_index("epoch")
    second = my_index(pairs, pair, 1)
    inside = (second >= begin) & (second < begin + 2)
    return my_index(pairs, pair, 0) - begin, (second & 1) + jnp.where(inside, 0, 2)


def references_kernel(
    pairs, images, powers, mine, bands, edge_bands, far_band, slots, scale, products
):
    for pair in range(4):
        band = column_band(look(pairs, pair, 1))
        bands[pair, : 4 * LANES, :] = band
        bands[pair, 4 * LANES :, :] = band
        edge_bands[pair] = row_band(look(pairs, pair, 0), PADDED, lambda k: k - HALO)
        window = (2 * look(pairs, pair, 0) + 1) * (2 * look(pairs, pair, 1) + 1)
        scale[pair] = 1.0 / jnp.full((HALO, 2 * LANES), window.astype(F32), F32)
        for k, slot in enumerate(near_slots(pairs, pair)):
            slots[pair, k] = jnp.full((HALO, LANES), slot.astype(F32), F32)
    far_band[...] = row_band(look(pairs, 1, 0), ROWS - 2 * HALO, lambda k: k + HALO)
    for pair in range(4):
        first = my_index(pairs, pair, 0) - 2 * lax.axis_index("epoch")
        for column in range(BLOCKS):
            at = block(column)
            a, b = (images[first, field, :, at].astype(F32) for field in range(2))
            put_split(products, pair, at, a * a + b * b)
        band = row_band(look(pairs, pair, 0), ROWS, lambda k: k)
        powers[pair] = row_sums(band, products[pair])
    first = my_index(pairs, 1, 0) - 2 * lax.axis_index("epoch")
    for column in range(BLOCKS):
        at = block(column)
        for field in range(2):
            mine[field, :, at] = images[first, field, :, at].astype(F32)[HALO : ROWS - HALO]


def interior_kernel(pairs, images, _, inner, own_up, own_down, own_columns):
    lead = asked(pairs)
    for column in range(BLOCKS):
        at = block(column)
        for field in range(2):
            values = images[lead, field, :, at].astype(F32)
            inner[field, :, at] = values[HALO : ROWS - HALO].astype(BF16)
    for a in range(2):
        rows = pl.ds(a * 16, 16)
        for column in range(BLOCKS):
            at = block(column)
            tops, bottoms = [], []
            for field in range(2):
                tops.append(images[a, field, :16, at].astype(F32)[:HALO])
                bottoms.append(images[a, field, ROWS - 16 :, at].astype(F32)[HALO:])
            own_up[rows, at] = jnp.concatenate(tops, axis=0).astype(BF16)
            own_down[rows, at] = jnp.concatenate(bottoms, axis=0).astype(BF16)
        for field in range(2):
            own_columns[2 * a + field, :, block(0)] = images[a, field, :, block(0)]
            own_columns[2 * a + field, :, block(1)] = images[a, field, :, block(BLOCKS - 1)]


def far_fields(a, b, c, d):
    return a * c + b * d, b * c - a * d, c * c + d * d


def near_rows_kernel(pairs, images, one, other, partial, held, products):
    held[:2] = images[...]
    for column in range(BLOCKS):
        at = block(column)
        for k in range(2):
            for field in range(2):
                values = next_rows(one, other, k, field, slice(0, ROWS), column)
                held[2 + k, field, :, at] = values.astype(BF16)

    def one_pair(step, carry):
        pair = jnp.where(step == 0, 0, step + 1)
        first, second = near_slots(pairs, pair)
        for column in range(BLOCKS):
            at = block(column)
            a, b = (held[first, field, :, at].astype(F32) for field in range(2))
            c, d = (held[second, field, :, at].astype(F32) for field in range(2))
            for f, value in enumerate(far_fields(a, b, c, d)):
                put_split(products, f, at, value)
        band = row_band(look(pairs, pair, 0), ROWS, lambda k: k)
        for f in range(3):
            partial[3 * step + f] = row_sums(band, products[f])
        return carry

    lax.fori_loop(0, 3, one_pair, 0)


def pack_rows_kernel(own_up, own_down, one, other, border, _, up, down):
    up[:32, :] = own_up[...]
    down[:32, :] = own_down[...]
    for column in range(BLOCKS):
        at = block(column)
        for k in range(2):
            tops, bottoms = [], []
            for field in range(2):
                tops.append(next_rows(one, other, k, field, slice(0, 16), column)[:HALO])
                bottoms.append(
                    next_rows(one, other, k, field, slice(ROWS - 16, ROWS), column)[HALO:]
                )
            rows = pl.ds(32 + 16 * k, 16)
            up[rows, at] = jnp.concatenate(tops, axis=0).astype(BF16)
            down[rows, at] = jnp.concatenate(bottoms, axis=0).astype(BF16)
        real = border[pl.ds(column * 32, 16), :].astype(F32)
        imag = border[pl.ds(column * 32 + 16, 16), :].astype(F32)
        up[64:, at] = jnp.concatenate([real[:HALO], imag[:HALO]], axis=0).astype(BF16)
        down[64:, at] = jnp.concatenate([real[HALO:], imag[HALO:]], axis=0).astype(BF16)


def halo_rows(above, below, acquisition, field, column):
    at = pl.ds(acquisition * 16, 16)
    rows = slice(field * HALO, (field + 1) * HALO)
    return (
        above[at, block(column)].astype(F32)[rows],
        below[at, block(column)].astype(F32)[rows],
    )


def pack_columns_kernel(own_columns, one, other, border, above, below, _, left, right):
    strips = border[pl.ds(BLOCKS * 32, 16), :].astype(F32)
    for side, column, ref in ((0, 0, left), (1, BLOCKS - 1, right)):
        total = jnp.zeros((PADDED, LANES), F32)
        source = side * (LANES - HALO)
        for acquisition in range(5):
            for field in range(2):
                before, after = halo_rows(above, below, acquisition, field, column)
                if acquisition < 2:
                    main = own_columns[2 * acquisition + field, :, block(side)].astype(F32)
                elif acquisition < 4:
                    main = next_rows(one, other, acquisition - 2, field, slice(0, ROWS), column)
                else:
                    rows = border[pl.ds(column * 32 + field * 16, 16), :].astype(F32)
                    inner = [
                        move_strip(strips, far_lane(part, field, side), source)
                        for part in range(3)
                    ]
                    main = jnp.concatenate([rows[:HALO], *inner, rows[HALO:]], axis=0)
                values = jnp.concatenate([before, main, after], axis=0)
                total = put_strip(total, values, source, HALO * (2 * acquisition + field))
        ref[...] = total.astype(BF16)


def halo_block(from_left, from_right, acquisition, field):
    source = HALO * (2 * acquisition + field)
    blank = jnp.zeros((PADDED, LANES), F32)
    after = put_strip(blank, from_right[...].astype(F32), source, 0)
    return put_strip(after, from_left[...].astype(F32), source, LANES - HALO)


def column_sums(j, band, rows, edges):
    begin, end = max(j * 256 - LANES, 0), min(j * 256 + 3 * LANES, COLS)
    parts = []
    for term in range(2):
        if j == 0:
            parts.append(edges(term))
        parts.append(rows(term, slice(begin, end)))
        if j == BLOCKS // 2 - 1:
            parts.append(edges(term))
    both = row_sums(jnp.concatenate(parts, axis=1), band)
    return [both[f : f + ROWS] for f in range(0, both.shape[0], ROWS)]


def put_terms(target, f, value, columns=slice(None)):
    high = value.astype(BF16)
    at = pl.ds(f * ROWS, ROWS)
    target[0, at, columns] = high
    target[1, at, columns] = (value - high.astype(F32)).astype(BF16)


def result_copies(pair, slot, j, held, interferogram, coherence, done):
    at = pl.ds(j * 256, 256)
    return (
        pltpu.make_async_copy(
            held.at[slot, pl.ds(0, 2), :, at],
            interferogram.at[pair, :, :, at],
            done.at[slot, j, 0],
        ),
        pltpu.make_async_copy(
            held.at[slot, 2, :, at], coherence.at[pair, :, at], done.at[slot, j, 1]
        ),
    )


def finish(real, imag, power, other, scale, pair, slot, j, results):
    held = results[0]
    scale = jnp.concatenate([scale] * (ROWS // HALO), axis=0)
    at = slice(j * 256, (j + 1) * 256)
    held[slot, 0, :, at] = real * scale
    held[slot, 1, :, at] = imag * scale
    held[slot, 2, :, at] = jnp.sqrt(real * real + imag * imag) / jnp.sqrt(power * other)
    for copy in result_copies(pair, slot, j, *results):
        copy.start()


def wait_for_results(pair, slot, results):
    for j in range(BLOCKS // 2):
        for copy in result_copies(pair, slot, j, *results):
            copy.wait()


def two_rows(upper, lower, acquisition, at):
    rows = pl.ds(pl.multiple_of(acquisition * 16, 16), 16)
    first, last = upper[rows, at].astype(F32), lower[rows, at].astype(F32)
    return (
        jnp.concatenate([first[:HALO], last[:HALO]], axis=0),
        jnp.concatenate([first[HALO:], last[HALO:]], axis=0),
    )


def power_of(a, b):
    return (a * a + b * b,)


def halo_rows_kernel(
    pairs, powers, partial, own_up, own_down, border, above, below, terms, far_partial, products
):
    def add(slots, half_rows, fields, place, main):
        for column in range(BLOCKS):
            at = block(column)
            values = [v for slot in slots for v in two_rows(above, below, slot, at)]
            for f, value in enumerate(fields(*values)):
                put_split(products, f, at, value)
        band = row_band(half_rows, 16, border_row)
        for f, value in enumerate(main):
            put_terms(terms, place + f, value() + row_sums(band, products[f, :32, :]))

    def one_pair(step, carry):
        pair = jnp.where(step == 0, 0, step + 1)
        main = (
            lambda: partial[3 * step],
            lambda: partial[3 * step + 1],
            lambda: powers[pair],
            lambda: partial[3 * step + 2],
        )
        add(near_slots(pairs, pair), look(pairs, pair, 0), fields_of, 4 * step, main)
        return carry

    lax.fori_loop(0, 3, one_pair, 0)
    first = my_index(pairs, 1, 0) - 2 * lax.axis_index("epoch")
    half_rows = look(pairs, 1, 0)
    add((first,), half_rows, power_of, 12, (lambda: powers[1],))
    for column in range(BLOCKS):
        at = block(column)
        outside = two_rows(above, below, first, at)
        inside = two_rows(own_up, own_down, first, at)
        values = [
            jnp.concatenate([o[:HALO], i, o[HALO:]], axis=0)
            for o, i in zip(outside, inside, strict=True)
        ]
        outside = two_rows(above, below, 4, at)
        for field in range(2):
            inside = border[pl.ds(column * 32 + field * 16, 16), :].astype(F32)
            values.append(
                jnp.concatenate([outside[field][:HALO], inside, outside[field][HALO:]], axis=0)
            )
        for f, value in enumerate(far_fields(*values)):
            put_split(products, f, at, value)
    band = row_band(half_rows, 32, wide_border_row)
    for f in range(3):
        far_partial[f] = row_sums(band, products[f])


def near_kernel(
    bands, edge_bands, slots, scale, terms, from_left, from_right,
    interferogram, coherence, far_power, far_edges,
    halos, products, edges, held, done,
):
    for acquisition in range(5):
        for field in range(2):
            halos[acquisition, field] = halo_block(from_left, from_right, acquisition, field)
    results = held, interferogram, coherence, done
    everything = slice(0, LANES)

    def halo_of(pair, k, field):
        slot = jnp.concatenate([slots[pair, k]] * (PADDED // HALO), axis=0)
        value = halos[0, field]
        for other in range(1, 4 if k else 2):
            value = jnp.where(slot == other, halos[other, field], value)
        return value

    def edge(target, values, pair, fields):
        for f, value in enumerate(fields(*values)):
            put_split(products, f, everything, value)
            put_terms(target, f, row_sums(edge_bands[pair], products[f]))

    def one_pair(step, carry):
        pair = jnp.where(step == 0, 0, step + 1)
        values = [halo_of(pair, k, field) for k in range(2) for field in range(2)]
        edge(edges, values, pair, fields_of)
        at = pl.ds(pl.multiple_of(step * 4 * ROWS, 4 * ROWS), 4 * ROWS)
        for j in range(BLOCKS // 2):
            blocks = column_sums(
                j, bands[pair], lambda term, columns: terms[term, at, columns], lambda term: edges[term]
            )
            finish(*blocks, scale[pair], pair, step, j, results)
        return carry

    lax.fori_loop(0, 3, one_pair, 0)

    reference = [halo_of(1, 0, field) for field in range(2)]
    edge(edges, reference, 1, power_of)
    for j in range(BLOCKS // 2):
        (far_power[:, j * 256 : (j + 1) * 256],) = column_sums(
            j,
            bands[1],
            lambda term, columns: terms[term, 12 * ROWS :, columns],
            lambda term: edges[term, :ROWS, :],
        )
    edge(far_edges, [*reference, halos[4, 0], halos[4, 1]], 1, far_fields)
    for step, pair in enumerate((0, 2, 3)):
        wait_for_results(pair, step, results)


def far_kernel(
    bands, band, scale, mine, inner, far_power, far_partial, far_edges, _, __,
    interferogram, coherence, products, terms, held, done,
):
    results = held, interferogram, coherence, done

    def rows(j):
        for column in (2 * j, 2 * j + 1):
            at = block(column)
            a, b = mine[0, :, at], mine[1, :, at]
            c, d = (inner[field, :, at].astype(F32) for field in range(2))
            for f, value in enumerate(far_fields(a, b, c, d)):
                put_split(products, f, at, value)
        at = slice(j * 256, (j + 1) * 256)
        for f in range(3):
            put_terms(terms, f, far_partial[f, :, at] + row_sums(band[...], products[f, :, at]), at)

    def columns(j):
        real, imag, other = column_sums(
            j, bands[1], lambda term, at: terms[term, :, at], lambda term: far_edges[term]
        )
        power = far_power[:, j * 256 : (j + 1) * 256]
        finish(real, imag, power, other, scale[1], 1, 0, j, results)

    rows(0)
    for j in range(1, BLOCKS // 2):
        rows(j)
        columns(j - 1)
    columns(BLOCKS // 2 - 1)
    wait_for_results(1, 0, results)


VMEM = pl.BlockSpec(memory_space=pltpu.VMEM)
SMEM = pl.BlockSpec(memory_space=pltpu.SMEM)
ANY = pl.BlockSpec(memory_space=pl.ANY)
PARAMS = pltpu.CompilerParams(vmem_limit_bytes=VMEM_LIMIT)


def shape(dims, dtype=BF16):
    return jax.ShapeDtypeStruct(dims, dtype)


def exchange(first, last, axis):
    peers = lax.axis_size(axis)
    up = [(i, i + 1) for i in range(peers - 1)]
    down = [(j, i) for i, j in up]
    return lax.ppermute(last, axis, up), lax.ppermute(first, axis, down)


def local(kernel, operands, places, results, name, kept=None, held=(), aliases=None, flops=0):
    return pl.pallas_call(
        kernel,
        in_specs=places,
        out_specs=kept or [VMEM] * len(results),
        out_shape=results,
        scratch_shapes=list(held),
        input_output_aliases=aliases or {},
        compiler_params=PARAMS,
        cost_estimate=pl.CostEstimate(flops=flops, bytes_accessed=0, transcendentals=0),
        name=name,
    )(*operands)


def body(slc_images, pair_list, look_sizes):
    groups = lax.axis_size("epoch")
    swap = [(b, (b + groups // 2) % groups) for b in range(groups)]
    table = jnp.concatenate([pair_list.T, look_sizes.T], axis=1)

    one = lax.ppermute(slc_images, "epoch", [(b + 1, b) for b in range(groups - 1)])
    border, images = local(
        split_kernel,
        (table, slc_images),
        [SMEM, VMEM],
        [shape((BLOCKS * 32 + 16, LANES)), shape((2, 2, ROWS, COLS))],
        "split",
    )
    border = lax.ppermute(border, "epoch", swap)
    powers, mine, bands, edge_bands, far_band, slots, scale = local(
        references_kernel,
        (table, images),
        [SMEM, VMEM],
        [
            shape((4, ROWS, COLS), F32),
            shape((2, ROWS - 2 * HALO, COLS), F32),
            shape((4, 8 * LANES, 2 * LANES)),
            shape((4, ROWS, 2 * PADDED)),
            shape((ROWS, 2 * (ROWS - 2 * HALO))),
            shape((4, 2, HALO, LANES), F32),
            shape((4, HALO, 2 * LANES), F32),
        ],
        "references",
        held=[pltpu.VMEM((4, 2 * ROWS, COLS), BF16)],
        flops=WORK,
    )
    inner, own_up, own_down, own_columns = local(
        interior_kernel,
        (table, images, powers),
        [SMEM, VMEM, VMEM],
        [
            shape((2, ROWS - 2 * HALO, COLS)),
            shape((32, COLS)),
            shape((32, COLS)),
            shape((4, ROWS, 2 * LANES)),
        ],
        "interior",
        flops=WORK,
    )
    inner = lax.ppermute(inner, "epoch", swap)
    other = lax.ppermute(images, "epoch", [(groups - 2, groups - 1)])

    up, down = local(
        pack_rows_kernel,
        (own_up, own_down, one, other, border, powers),
        [VMEM] * 6,
        [shape((80, COLS))] * 2,
        "pack_rows",
    )
    above, below = exchange(up, down, "row")
    (partial,) = local(
        near_rows_kernel,
        (table, images, one, other),
        [SMEM] + [VMEM] * 3,
        [shape((9, ROWS, COLS), F32)],
        "near_rows",
        held=[
            pltpu.VMEM((4, 2, ROWS, COLS), BF16),
            pltpu.VMEM((3, 2 * ROWS, COLS), BF16),
        ],
        flops=LITTLE,
    )
    left, right = local(
        pack_columns_kernel,
        (own_columns, one, other, border, above, below, partial),
        [VMEM] * 7,
        [shape((PADDED, LANES))] * 2,
        "pack_columns",
    )
    from_left, from_right = exchange(left, right, "col")
    terms, rest = local(
        halo_rows_kernel,
        (table, powers, partial, own_up, own_down, border, above, below),
        [SMEM] + [VMEM] * 7,
        [shape((2, 13 * ROWS, COLS)), shape((3, ROWS, COLS), F32)],
        "halo_rows",
        held=[pltpu.VMEM((4, 64, COLS), BF16)],
        flops=LITTLE,
    )

    outs = [shape((4, 2, ROWS, COLS), F32), shape((4, ROWS, COLS), F32)]
    interferogram, coherence, power, edges = local(
        near_kernel,
        (bands, edge_bands, slots, scale, terms, from_left, from_right),
        [VMEM] * 7,
        [*outs, shape((ROWS, COLS), F32), shape((2, 3 * ROWS, LANES))],
        "near_pairs",
        kept=[ANY, ANY, VMEM, VMEM],
        held=[
            pltpu.VMEM((5, 2, PADDED, LANES), F32),
            pltpu.VMEM((4, 2 * PADDED, LANES), BF16),
            pltpu.VMEM((2, 4 * ROWS, LANES), BF16),
            pltpu.VMEM((3, 3, ROWS, COLS), F32),
            pltpu.SemaphoreType.DMA((3, BLOCKS // 2, 2)),
        ],
    )
    return local(
        far_kernel,
        (bands, far_band, scale, mine, inner, power, rest, edges, interferogram, coherence),
        [VMEM] * 8 + [ANY] * 2,
        outs,
        "far_pair",
        kept=[ANY, ANY],
        held=[
            pltpu.VMEM((3, 2 * (ROWS - 2 * HALO), COLS), BF16),
            pltpu.VMEM((2, 3 * ROWS, COLS), BF16),
            pltpu.VMEM((1, 3, ROWS, COLS), F32),
            pltpu.SemaphoreType.DMA((1, BLOCKS // 2, 2)),
        ],
        aliases={8: 0, 9: 1},
    )


def solution(mesh):
    placed = (P("epoch", None, "row", "col"), P(), P("epoch", None))
    return jax.shard_map(
        body,
        mesh=mesh,
        in_specs=placed,
        out_specs=(P("epoch", None, "row", "col"), P("epoch", "row", "col")),
        check_vma=False,
    )
```

```python
import jax
import jax.numpy as jnp
from jax import lax
from jax.experimental import pallas as pl
from jax.experimental.pallas import tpu as pltpu
from jax.sharding import PartitionSpec as P

HALO = 8
LANES = 128
ROWS = 64
COLS = 1024
BLOCKS = COLS // LANES
PADDED = ROWS + 2 * HALO
F32 = jnp.float32
BF16 = jnp.bfloat16
WORK = 20_000_000_000
LITTLE = 100_000_000
VMEM_LIMIT = 24 * 1024 * 1024


def lane_iota(rows):
    return lax.broadcasted_iota(jnp.int32, (rows, LANES), 1)


def move_strip(values, source, target):
    return pltpu.roll(values, (target - source) % LANES, 1)


def put_strip(total, values, source, target):
    lane = lane_iota(values.shape[0])
    inside = (lane >= target) & (lane < target + HALO)
    return jnp.where(inside, move_strip(values, source, target), total)


def block(index):
    return slice(index * LANES, (index + 1) * LANES)


def far_lane(part, field, side):
    return HALO * (part * 4 + field * 2 + side)


def my_index(pairs, pair, which):
    return pairs[which, 4 * lax.axis_index("epoch") + pair]


def look(pairs, pair, which):
    return pairs[which, 4 * lax.axis_size("epoch") + pair]


def is_last():
    return lax.axis_index("epoch") == lax.axis_size("epoch") - 1


def asked(pairs):
    groups = lax.axis_size("epoch")
    myself = lax.axis_index("epoch")
    asker = lax.rem(myself + groups // 2, groups)
    return pairs[1, 4 * asker + 1] - 2 * myself


def split_kernel(pairs, images, border, kept):
    kept[...] = images[...]
    lead = asked(pairs)

    def chosen(field, rows, column):
        return images[lead, field, rows, block(column)].astype(F32)

    strips = jnp.zeros((16, LANES), F32)
    for column in range(BLOCKS):
        for field in range(2):
            first = chosen(field, slice(0, 16), column)
            last = chosen(field, slice(ROWS - 16, ROWS), column)
            rows = jnp.concatenate([first[:HALO], last[HALO:]], axis=0)
            border[pl.ds(column * 32 + field * 16, 16), :] = rows.astype(BF16)
            for side, at in ((0, 0), (1, BLOCKS - 1)):
                if column == at:
                    values = chosen(field, slice(0, ROWS), column)
                    for part in range(3):
                        begin = HALO + 16 * part
                        strips = put_strip(
                            strips,
                            values[begin : begin + 16],
                            side * (LANES - HALO),
                            far_lane(part, field, side),
                        )
    border[pl.ds(BLOCKS * 32, 16), :] = strips.astype(BF16)


def next_rows(one, other, k, field, rows, column):
    at = block(column)
    return one[k, field, rows, at].astype(F32) + other[k, field, rows, at].astype(F32)


def fields_of(a, b, c, d):
    return a * c + b * d, b * c - a * d, a * a + b * b, c * c + d * d


def put_split(target, f, at, value):
    count = value.shape[0]
    high = value.astype(BF16)
    target[f, :count, at] = high
    target[f, count : 2 * count, at] = (value - high.astype(F32)).astype(BF16)


def row_band(half_rows, count, row_of):
    inner = lax.broadcasted_iota(jnp.int32, (ROWS, 2 * count), 0)
    outer = lax.broadcasted_iota(jnp.int32, (ROWS, 2 * count), 1)
    outer = row_of(jnp.where(outer >= count, outer - count, outer))
    return (jnp.abs(outer - inner) <= half_rows).astype(F32).astype(BF16)


def border_row(k):
    return jnp.where(k < HALO, k - HALO, k + ROWS - HALO)


def wide_border_row(k):
    return jnp.where(k < 16, k - HALO, k + ROWS - 3 * HALO)


def row_sums(band, products):
    return jnp.dot(band, products, preferred_element_type=F32)


def column_band(half_cols):
    outer = lax.broadcasted_iota(jnp.int32, (4 * LANES, 2 * LANES), 0)
    inner = lax.broadcasted_iota(jnp.int32, (4 * LANES, 2 * LANES), 1)
    return (jnp.abs(outer - LANES - inner) <= half_cols).astype(F32).astype(BF16)


def near_slots(pairs, pair):
    begin = 2 * lax.axis_index("epoch")
    second = my_index(pairs, pair, 1)
    inside = (second >= begin) & (second < begin + 2)
    return my_index(pairs, pair, 0) - begin, (second & 1) + jnp.where(inside, 0, 2)


def references_kernel(
    pairs, images, powers, mine, bands, edge_bands, far_band, slots, scale, products
):
    for pair in range(4):
        band = column_band(look(pairs, pair, 1))
        bands[pair, : 4 * LANES, :] = band
        bands[pair, 4 * LANES :, :] = band
        edge_bands[pair] = row_band(look(pairs, pair, 0), PADDED, lambda k: k - HALO)
        window = (2 * look(pairs, pair, 0) + 1) * (2 * look(pairs, pair, 1) + 1)
        scale[pair] = 1.0 / jnp.full((HALO, 2 * LANES), window.astype(F32), F32)
        for k, slot in enumerate(near_slots(pairs, pair)):
            slots[pair, k] = jnp.full((HALO, LANES), slot.astype(F32), F32)
    far_band[...] = row_band(look(pairs, 1, 0), ROWS - 2 * HALO, lambda k: k + HALO)
    for pair in range(4):
        first = my_index(pairs, pair, 0) - 2 * lax.axis_index("epoch")
        for column in range(BLOCKS):
            at = block(column)
            a, b = (images[first, field, :, at].astype(F32) for field in range(2))
            put_split(products, pair, at, a * a + b * b)
        band = row_band(look(pairs, pair, 0), ROWS, lambda k: k)
        powers[pair] = row_sums(band, products[pair])
    first = my_index(pairs, 1, 0) - 2 * lax.axis_index("epoch")
    for column in range(BLOCKS):
        at = block(column)
        for field in range(2):
            mine[field, :, at] = images[first, field, :, at].astype(F32)[HALO : ROWS - HALO]


def interior_kernel(pairs, images, _, inner, own_up, own_down, own_columns):
    lead = asked(pairs)
    for column in range(BLOCKS):
        at = block(column)
        for field in range(2):
            values = images[lead, field, :, at].astype(F32)
            inner[field, :, at] = values[HALO : ROWS - HALO].astype(BF16)
    for a in range(2):
        rows = pl.ds(a * 16, 16)
        for column in range(BLOCKS):
            at = block(column)
            tops, bottoms = [], []
            for field in range(2):
                tops.append(images[a, field, :16, at].astype(F32)[:HALO])
                bottoms.append(images[a, field, ROWS - 16 :, at].astype(F32)[HALO:])
            own_up[rows, at] = jnp.concatenate(tops, axis=0).astype(BF16)
            own_down[rows, at] = jnp.concatenate(bottoms, axis=0).astype(BF16)
        for field in range(2):
            own_columns[2 * a + field, :, block(0)] = images[a, field, :, block(0)]
            own_columns[2 * a + field, :, block(1)] = images[a, field, :, block(BLOCKS - 1)]


def far_fields(a, b, c, d):
    return a * c + b * d, b * c - a * d, c * c + d * d


def near_rows_kernel(pairs, images, one, other, partial, held, products):
    held[:2] = images[...]
    for column in range(BLOCKS):
        at = block(column)
        for k in range(2):
            for field in range(2):
                values = next_rows(one, other, k, field, slice(0, ROWS), column)
                held[2 + k, field, :, at] = values.astype(BF16)

    def one_pair(step, carry):
        pair = jnp.where(step == 0, 0, step + 1)
        first, second = near_slots(pairs, pair)
        for column in range(BLOCKS):
            at = block(column)
            a, b = (held[first, field, :, at].astype(F32) for field in range(2))
            c, d = (held[second, field, :, at].astype(F32) for field in range(2))
            for f, value in enumerate(far_fields(a, b, c, d)):
                put_split(products, f, at, value)
        band = row_band(look(pairs, pair, 0), ROWS, lambda k: k)
        for f in range(3):
            partial[3 * step + f] = row_sums(band, products[f])
        return carry

    lax.fori_loop(0, 3, one_pair, 0)


def pack_rows_kernel(own_up, own_down, one, other, border, _, up, down):
    up[:32, :] = own_up[...]
    down[:32, :] = own_down[...]
    for column in range(BLOCKS):
        at = block(column)
        for k in range(2):
            tops, bottoms = [], []
            for field in range(2):
                tops.append(next_rows(one, other, k, field, slice(0, 16), column)[:HALO])
                bottoms.append(
                    next_rows(one, other, k, field, slice(ROWS - 16, ROWS), column)[HALO:]
                )
            rows = pl.ds(32 + 16 * k, 16)
            up[rows, at] = jnp.concatenate(tops, axis=0).astype(BF16)
            down[rows, at] = jnp.concatenate(bottoms, axis=0).astype(BF16)
        real = border[pl.ds(column * 32, 16), :].astype(F32)
        imag = border[pl.ds(column * 32 + 16, 16), :].astype(F32)
        up[64:, at] = jnp.concatenate([real[:HALO], imag[:HALO]], axis=0).astype(BF16)
        down[64:, at] = jnp.concatenate([real[HALO:], imag[HALO:]], axis=0).astype(BF16)


def halo_rows(above, below, acquisition, field, column):
    at = pl.ds(acquisition * 16, 16)
    rows = slice(field * HALO, (field + 1) * HALO)
    return (
        above[at, block(column)].astype(F32)[rows],
        below[at, block(column)].astype(F32)[rows],
    )


def pack_columns_kernel(own_columns, one, other, border, above, below, _, left, right):
    strips = border[pl.ds(BLOCKS * 32, 16), :].astype(F32)
    for side, column, ref in ((0, 0, left), (1, BLOCKS - 1, right)):
        total = jnp.zeros((PADDED, LANES), F32)
        source = side * (LANES - HALO)
        for acquisition in range(5):
            for field in range(2):
                before, after = halo_rows(above, below, acquisition, field, column)
                if acquisition < 2:
                    main = own_columns[2 * acquisition + field, :, block(side)].astype(F32)
                elif acquisition < 4:
                    main = next_rows(one, other, acquisition - 2, field, slice(0, ROWS), column)
                else:
                    rows = border[pl.ds(column * 32 + field * 16, 16), :].astype(F32)
                    inner = [
                        move_strip(strips, far_lane(part, field, side), source)
                        for part in range(3)
                    ]
                    main = jnp.concatenate([rows[:HALO], *inner, rows[HALO:]], axis=0)
                values = jnp.concatenate([before, main, after], axis=0)
                total = put_strip(total, values, source, HALO * (2 * acquisition + field))
        ref[...] = total.astype(BF16)


def halo_block(from_left, from_right, acquisition, field):
    source = HALO * (2 * acquisition + field)
    blank = jnp.zeros((PADDED, LANES), F32)
    after = put_strip(blank, from_right[...].astype(F32), source, 0)
    return put_strip(after, from_left[...].astype(F32), source, LANES - HALO)


def column_sums(j, band, rows, edges):
    begin, end = max(j * 256 - LANES, 0), min(j * 256 + 3 * LANES, COLS)
    parts = []
    for term in range(2):
        if j == 0:
            parts.append(edges(term))
        parts.append(rows(term, slice(begin, end)))
        if j == BLOCKS // 2 - 1:
            parts.append(edges(term))
    both = row_sums(jnp.concatenate(parts, axis=1), band)
    return [both[f : f + ROWS] for f in range(0, both.shape[0], ROWS)]


def put_terms(target, f, value, columns=slice(None)):
    high = value.astype(BF16)
    at = pl.ds(f * ROWS, ROWS)
    target[0, at, columns] = high
    target[1, at, columns] = (value - high.astype(F32)).astype(BF16)


def result_copies(pair, slot, j, held, interferogram, coherence, done):
    at = pl.ds(j * 256, 256)
    return (
        pltpu.make_async_copy(
            held.at[slot, pl.ds(0, 2), :, at],
            interferogram.at[pair, :, :, at],
            done.at[slot, j, 0],
        ),
        pltpu.make_async_copy(
            held.at[slot, 2, :, at], coherence.at[pair, :, at], done.at[slot, j, 1]
        ),
    )


def finish(real, imag, power, other, scale, pair, slot, j, results):
    held = results[0]
    scale = jnp.concatenate([scale] * (ROWS // HALO), axis=0)
    at = slice(j * 256, (j + 1) * 256)
    held[slot, 0, :, at] = real * scale
    held[slot, 1, :, at] = imag * scale
    held[slot, 2, :, at] = jnp.sqrt(real * real + imag * imag) / jnp.sqrt(power * other)
    for copy in result_copies(pair, slot, j, *results):
        copy.start()


def wait_for_results(pair, slot, results):
    for j in range(BLOCKS // 2):
        for copy in result_copies(pair, slot, j, *results):
            copy.wait()


def two_rows(upper, lower, acquisition, at):
    rows = pl.ds(pl.multiple_of(acquisition * 16, 16), 16)
    first, last = upper[rows, at].astype(F32), lower[rows, at].astype(F32)
    return (
        jnp.concatenate([first[:HALO], last[:HALO]], axis=0),
        jnp.concatenate([first[HALO:], last[HALO:]], axis=0),
    )


def power_of(a, b):
    return (a * a + b * b,)


def halo_rows_kernel(
    pairs, powers, partial, own_up, own_down, border, above, below, terms, far_partial, products
):
    def add(slots, half_rows, fields, place, main):
        for column in range(BLOCKS):
            at = block(column)
            values = [v for slot in slots for v in two_rows(above, below, slot, at)]
            for f, value in enumerate(fields(*values)):
                put_split(products, f, at, value)
        band = row_band(half_rows, 16, border_row)
        for f, value in enumerate(main):
            put_terms(terms, place + f, value() + row_sums(band, products[f, :32, :]))

    def one_pair(step, carry):
        pair = jnp.where(step == 0, 0, step + 1)
        main = (
            lambda: partial[3 * step],
            lambda: partial[3 * step + 1],
            lambda: powers[pair],
            lambda: partial[3 * step + 2],
        )
        add(near_slots(pairs, pair), look(pairs, pair, 0), fields_of, 4 * step, main)
        return carry

    lax.fori_loop(0, 3, one_pair, 0)
    first = my_index(pairs, 1, 0) - 2 * lax.axis_index("epoch")
    half_rows = look(pairs, 1, 0)
    add((first,), half_rows, power_of, 12, (lambda: powers[1],))
    for column in range(BLOCKS):
        at = block(column)
        outside = two_rows(above, below, first, at)
        inside = two_rows(own_up, own_down, first, at)
        values = [
            jnp.concatenate([o[:HALO], i, o[HALO:]], axis=0)
            for o, i in zip(outside, inside, strict=True)
        ]
        outside = two_rows(above, below, 4, at)
        for field in range(2):
            inside = border[pl.ds(column * 32 + field * 16, 16), :].astype(F32)
            values.append(
                jnp.concatenate([outside[field][:HALO], inside, outside[field][HALO:]], axis=0)
            )
        for f, value in enumerate(far_fields(*values)):
            put_split(products, f, at, value)
    band = row_band(half_rows, 32, wide_border_row)
    for f in range(3):
        far_partial[f] = row_sums(band, products[f])


def near_kernel(
    bands, edge_bands, slots, scale, terms, from_left, from_right,
    interferogram, coherence, far_power, far_edges,
    halos, products, edges, held, done,
):
    for acquisition in range(5):
        for field in range(2):
            halos[acquisition, field] = halo_block(from_left, from_right, acquisition, field)
    results = held, interferogram, coherence, done
    everything = slice(0, LANES)

    def halo_of(pair, k, field):
        slot = jnp.concatenate([slots[pair, k]] * (PADDED // HALO), axis=0)
        value = halos[0, field]
        for other in range(1, 4 if k else 2):
            value = jnp.where(slot == other, halos[other, field], value)
        return value

    def edge(target, values, pair, fields):
        for f, value in enumerate(fields(*values)):
            put_split(products.at[pair], f, everything, value)
            put_terms(target, f, row_sums(edge_bands[pair], products[pair, f]))

    for step, pair in enumerate((0, 2, 3)):
        values = [halo_of(pair, k, field) for k in range(2) for field in range(2)]
        edge(edges.at[pair], values, pair, fields_of)
        at = slice(step * 4 * ROWS, (step + 1) * 4 * ROWS)
        for j in range(BLOCKS // 2):
            blocks = column_sums(
                j,
                bands[pair],
                lambda term, columns, at=at: terms[term, at, columns],
                lambda term, pair=pair: edges[pair, term],
            )
            finish(*blocks, scale[pair], pair, step, j, results)

    reference = [halo_of(1, 0, field) for field in range(2)]
    edge(edges.at[1], reference, 1, power_of)
    for j in range(BLOCKS // 2):
        (far_power[:, j * 256 : (j + 1) * 256],) = column_sums(
            j,
            bands[1],
            lambda term, columns: terms[term, 12 * ROWS :, columns],
            lambda term: edges[1, term, :ROWS, :],
        )
    edge(far_edges, [*reference, halos[4, 0], halos[4, 1]], 1, far_fields)
    for step, pair in enumerate((0, 2, 3)):
        wait_for_results(pair, step, results)


def far_kernel(
    bands, band, scale, mine, inner, far_power, far_partial, far_edges, _, __,
    interferogram, coherence, products, terms, held, done,
):
    results = held, interferogram, coherence, done

    def rows(j):
        for column in (2 * j, 2 * j + 1):
            at = block(column)
            a, b = mine[0, :, at], mine[1, :, at]
            c, d = (inner[field, :, at].astype(F32) for field in range(2))
            for f, value in enumerate(far_fields(a, b, c, d)):
                put_split(products, f, at, value)
        at = slice(j * 256, (j + 1) * 256)
        for f in range(3):
            put_terms(terms, f, far_partial[f, :, at] + row_sums(band[...], products[f, :, at]), at)

    def columns(j):
        real, imag, other = column_sums(
            j, bands[1], lambda term, at: terms[term, :, at], lambda term: far_edges[term]
        )
        power = far_power[:, j * 256 : (j + 1) * 256]
        finish(real, imag, power, other, scale[1], 1, 0, j, results)

    rows(0)
    for j in range(1, BLOCKS // 2):
        rows(j)
        columns(j - 1)
    columns(BLOCKS // 2 - 1)
    wait_for_results(1, 0, results)


VMEM = pl.BlockSpec(memory_space=pltpu.VMEM)
SMEM = pl.BlockSpec(memory_space=pltpu.SMEM)
ANY = pl.BlockSpec(memory_space=pl.ANY)
PARAMS = pltpu.CompilerParams(vmem_limit_bytes=VMEM_LIMIT)


def shape(dims, dtype=BF16):
    return jax.ShapeDtypeStruct(dims, dtype)


def exchange(first, last, axis):
    peers = lax.axis_size(axis)
    up = [(i, i + 1) for i in range(peers - 1)]
    down = [(j, i) for i, j in up]
    return lax.ppermute(last, axis, up), lax.ppermute(first, axis, down)


def local(kernel, operands, places, results, name, kept=None, held=(), aliases=None, flops=0):
    return pl.pallas_call(
        kernel,
        in_specs=places,
        out_specs=kept or [VMEM] * len(results),
        out_shape=results,
        scratch_shapes=list(held),
        input_output_aliases=aliases or {},
        compiler_params=PARAMS,
        cost_estimate=pl.CostEstimate(flops=flops, bytes_accessed=0, transcendentals=0),
        name=name,
    )(*operands)


def body(slc_images, pair_list, look_sizes):
    groups = lax.axis_size("epoch")
    swap = [(b, (b + groups // 2) % groups) for b in range(groups)]
    table = jnp.concatenate([pair_list.T, look_sizes.T], axis=1)

    one = lax.ppermute(slc_images, "epoch", [(b + 1, b) for b in range(groups - 1)])
    border, images = local(
        split_kernel,
        (table, slc_images),
        [SMEM, VMEM],
        [shape((BLOCKS * 32 + 16, LANES)), shape((2, 2, ROWS, COLS))],
        "split",
    )
    border = lax.ppermute(border, "epoch", swap)
    powers, mine, bands, edge_bands, far_band, slots, scale = local(
        references_kernel,
        (table, images),
        [SMEM, VMEM],
        [
            shape((4, ROWS, COLS), F32),
            shape((2, ROWS - 2 * HALO, COLS), F32),
            shape((4, 8 * LANES, 2 * LANES)),
            shape((4, ROWS, 2 * PADDED)),
            shape((ROWS, 2 * (ROWS - 2 * HALO))),
            shape((4, 2, HALO, LANES), F32),
            shape((4, HALO, 2 * LANES), F32),
        ],
        "references",
        held=[pltpu.VMEM((4, 2 * ROWS, COLS), BF16)],
        flops=WORK,
    )
    inner, own_up, own_down, own_columns = local(
        interior_kernel,
        (table, images, powers),
        [SMEM, VMEM, VMEM],
        [
            shape((2, ROWS - 2 * HALO, COLS)),
            shape((32, COLS)),
            shape((32, COLS)),
            shape((4, ROWS, 2 * LANES)),
        ],
        "interior",
        flops=WORK,
    )
    inner = lax.ppermute(inner, "epoch", swap)
    other = lax.ppermute(images, "epoch", [(groups - 2, groups - 1)])

    up, down = local(
        pack_rows_kernel,
        (own_up, own_down, one, other, border, powers),
        [VMEM] * 6,
        [shape((80, COLS))] * 2,
        "pack_rows",
    )
    above, below = exchange(up, down, "row")
    (partial,) = local(
        near_rows_kernel,
        (table, images, one, other),
        [SMEM] + [VMEM] * 3,
        [shape((9, ROWS, COLS), F32)],
        "near_rows",
        held=[
            pltpu.VMEM((4, 2, ROWS, COLS), BF16),
            pltpu.VMEM((3, 2 * ROWS, COLS), BF16),
        ],
        flops=LITTLE,
    )
    left, right = local(
        pack_columns_kernel,
        (own_columns, one, other, border, above, below, partial),
        [VMEM] * 7,
        [shape((PADDED, LANES))] * 2,
        "pack_columns",
    )
    from_left, from_right = exchange(left, right, "col")
    terms, rest = local(
        halo_rows_kernel,
        (table, powers, partial, own_up, own_down, border, above, below),
        [SMEM] + [VMEM] * 7,
        [shape((2, 13 * ROWS, COLS)), shape((3, ROWS, COLS), F32)],
        "halo_rows",
        held=[pltpu.VMEM((4, 64, COLS), BF16)],
        flops=LITTLE,
    )

    outs = [shape((4, 2, ROWS, COLS), F32), shape((4, ROWS, COLS), F32)]
    interferogram, coherence, power, edges = local(
        near_kernel,
        (bands, edge_bands, slots, scale, terms, from_left, from_right),
        [VMEM] * 7,
        [*outs, shape((ROWS, COLS), F32), shape((2, 3 * ROWS, LANES))],
        "near_pairs",
        kept=[ANY, ANY, VMEM, VMEM],
        held=[
            pltpu.VMEM((5, 2, PADDED, LANES), F32),
            pltpu.VMEM((4, 4, 2 * PADDED, LANES), BF16),
            pltpu.VMEM((4, 2, 4 * ROWS, LANES), BF16),
            pltpu.VMEM((3, 3, ROWS, COLS), F32),
            pltpu.SemaphoreType.DMA((3, BLOCKS // 2, 2)),
        ],
    )
    return local(
        far_kernel,
        (bands, far_band, scale, mine, inner, power, rest, edges, interferogram, coherence),
        [VMEM] * 8 + [ANY] * 2,
        outs,
        "far_pair",
        kept=[ANY, ANY],
        held=[
            pltpu.VMEM((3, 2 * (ROWS - 2 * HALO), COLS), BF16),
            pltpu.VMEM((2, 3 * ROWS, COLS), BF16),
            pltpu.VMEM((1, 3, ROWS, COLS), F32),
            pltpu.SemaphoreType.DMA((1, BLOCKS // 2, 2)),
        ],
        aliases={8: 0, 9: 1},
    )


def solution(mesh):
    placed = (P("epoch", None, "row", "col"), P(), P("epoch", None))
    return jax.shard_map(
        body,
        mesh=mesh,
        in_specs=placed,
        out_specs=(P("epoch", None, "row", "col"), P("epoch", "row", "col")),
        check_vma=False,
    )
```
